32 devices in a mesh: seq: 8 (over z, x), tm: 4 (over y, core).
Axes of the slice: x: 2, y: 2, z: 4, core: 2. Of those that a mesh axis runs over, the one named last changes fastest.
Arguments:
- latent: bfloat16 [8, 4096], P(None, ('seq', 'tm')), may hold values from -6 to 6
- first_kernel: bfloat16 [3, 3, 3, 16, 512], replicated, may hold values from -0.3125 to 0.3125
- first_bias: float32 [512], replicated, may hold values from -3 to 3
- first_gain: float32 [512], replicated, may hold values from 0.1 to 1.9
- second_kernel: bfloat16 [3, 3, 3, 512, 256], replicated, may hold values from -0.0546875 to 0.0546875
- second_bias: float32 [256], replicated, may hold values from -3 to 3
- second_gain: float32 [256], replicated, may hold values from 0.1 to 1.9
- final_kernel: bfloat16 [3, 3, 3, 256, 128], replicated, may hold values from -0.078125 to 0.078125
- final_bias: float32 [128], replicated, may hold values from -2 to 2
Outputs:
- decoded: bfloat16 [8, 32, 128, 128], P('tm', 'seq')
The draws below stay inside these ranges and needn't reach their ends.
All inputs are finite; a program needn't handle non-finite values.
Results may differ from the reference program's by a relative error of at most 0.0051.
Values may be sent and summed in bfloat16 or wider, within the bound.
No kernel may reach another device: no remote copies, remote signals or barrier semaphores. Data moves between devices by JAX's collectives and lax.ppermute only.
A program may use at most 64 MiB of HBM per device.

```python
import jax
import jax.numpy as jnp
from jax import lax

CL = 16
C1 = 512
C2 = 256
C3 = 128
W = 32
FRAMES = 8
ROWS = 8


def block_levels(key, dims, pieces, low, top_value):
    level, own = 1.0, jax.random.fold_in(key, 6)
    for dim, blocks in pieces:
        steps = jnp.exp(jax.random.uniform(jax.random.fold_in(own, dim), (blocks,), jnp.float32, low / len(pieces), top_value / len(pieces)))
        level = level * jnp.repeat(steps, dims[dim] // blocks).reshape([-1 if axis == dim else 1 for axis in range(len(dims))])
    return level


def normal_values(key, extent, deviation, most, pieces=(), held_as=jnp.bfloat16):
    gain = block_levels(key, extent, pieces, -0.22, 0.18) if pieces else 1.0
    entries = jax.random.normal(key, extent, jnp.float32) * deviation * gain
    return jnp.minimum(jnp.maximum(entries, -most), most).astype(held_as)


def setup_inputs(seed: int = 0) -> dict:
    seeds = jax.random.split(jax.random.key(seed), 10)
    return {
        "latent": normal_values(seeds[0], (FRAMES, ROWS * W * CL), 1.0, 6.0, ((1, 32),)),
        "first_kernel": normal_values(seeds[1], (3, 3, 3, CL, C1), (27 * CL) ** -0.5, 0.3125),
        "first_bias": normal_values(seeds[2], (C1,), 0.5, 3.0, (), jnp.float32),
        "first_gain": jnp.clip(1.0 + 0.18 * jax.random.normal(seeds[3], (C1,), jnp.float32), 0.1, 1.9),
        "second_kernel": normal_values(seeds[4], (3, 3, 3, C1, C2), (27 * C1) ** -0.5, 0.0546875),
        "second_bias": normal_values(seeds[5], (C2,), 0.5, 3.0, (), jnp.float32),
        "second_gain": jnp.clip(1.0 + 0.18 * jax.random.normal(seeds[6], (C2,), jnp.float32), 0.1, 1.9),
        "final_kernel": normal_values(seeds[7], (3, 3, 3, C2, C3), (27 * C2) ** -0.5, 0.078125),
        "final_bias": normal_values(seeds[8], (C3,), 0.3, 2.0, (), jnp.float32),
    }


def edge_conv(field, kernel, offset):
    padded = jnp.pad(field, ((2, 0), (1, 1), (1, 1), (0, 0)), mode='edge')
    result = lax.conv_general_dilated(padded[None], kernel.astype(jnp.float32), (1, 1, 1), 'VALID', dimension_numbers=('NDHWC', 'DHWIO', 'NDHWC'), precision=lax.Precision.HIGHEST)
    return result[0] + offset

def normed(hidden, norm_gain):
    factor = lax.rsqrt(lax.optimization_barrier(jnp.mean(hidden * hidden, axis=3, keepdims=True)) + 1e-06)
    return jax.nn.silu(hidden * factor * norm_gain).astype(jnp.bfloat16)

def enlarge(field):
    return jnp.repeat(jnp.repeat(field, 2, axis=1), 2, axis=2)

def reference(latent, first_kernel, first_bias, first_gain, second_kernel, second_bias, second_gain, final_kernel, final_bias):
    latent_grid = latent.reshape(FRAMES, ROWS, W, CL).astype(jnp.float32)
    first_act = normed(edge_conv(latent_grid, first_kernel, first_bias), first_gain)
    second_act = normed(edge_conv(enlarge(first_act.astype(jnp.float32)), second_kernel, second_bias), second_gain)
    decoded = edge_conv(enlarge(second_act.astype(jnp.float32)), final_kernel, final_bias)
    return decoded.astype(jnp.bfloat16)
```

```python
import functools

import jax
import jax.numpy as jnp
from jax import lax
from jax.experimental import pallas as pl
from jax.experimental.pallas import tpu as pltpu
from jax.sharding import PartitionSpec as P

F32, BF16 = jnp.float32, jnp.bfloat16
AXES = ("seq", "tm")


def hop(array, partner, seq, tm):
    pairs = []
    for s in range(seq):
        for t in range(tm):
            s2, t2 = partner(s, t)
            pairs.append((s * tm + t, s2 * tm + t2))
    return lax.ppermute(array, AXES, pairs)


def gathered_pieces(latent):
    seq, tm = lax.axis_size("seq"), lax.axis_size("tm")
    assert seq % 2 == 0 and tm == 4

    def z_partner(first):
        def partner(s, t):
            z = s // 2
            other = z + 1 if (z - first) % 2 == 0 else z - 1
            return (s + 2 * (other - z), t ^ 1) if 0 <= other < seq // 2 else (s, t ^ 1)

        return partner

    held = latent[None]
    held = jnp.concatenate([held, hop(held, lambda s, t: (s, t ^ 3), seq, tm)])
    held = jnp.concatenate([held, hop(held, lambda s, t: (s ^ 1, t ^ 1), seq, tm)])
    even = hop(held, z_partner(0), seq, tm)
    odd = hop(held, z_partner(1), seq, tm)
    held = jnp.concatenate([held, even, odd])
    return jnp.concatenate([held, hop(held, lambda s, t: (s, t ^ 1), seq, tm)])


def silu(v):
    return 0.5 * v * (1.0 + jnp.tanh(0.5 * v))


def normed(hidden, gain):
    factor = lax.rsqrt(jnp.mean(hidden * hidden, axis=-1, keepdims=True) + 1e-06)
    return silu(hidden * factor * gain).astype(BF16)


def decode_kernel(
    rows_total,
    pieces,
    w1,
    b1,
    g1,
    w2,
    b2,
    g2,
    w3,
    b3,
    out,
    rolled,
    rolled_far,
    patches,
    first_act,
    partial,
    second_act,
    final,
    line,
):
    s = lax.axis_index("seq")
    t = lax.axis_index("tm")
    z, x, y, c = s // 2, s % 2, t // 2, t % 2
    n_frames = pieces.shape[1]

    def piece_of(row, chunk):
        dz, dx = row // 2 - z, row % 2 ^ x
        dy, dc = chunk // 2 ^ y, chunk % 2 ^ c
        group = jnp.where(dz == 0, 0, jnp.where((dz == 1) == (z % 2 == 0), 1, 2))
        half = (dx + dy + dc + jnp.where(dz == 0, 0, 1)) % 2
        return half * 12 + group * 4 + 2 * dx + dy

    lane = lax.broadcasted_iota(jnp.int32, (n_frames, 128), 1)

    def one_row(d, _):
        row = jnp.clip(s - 2 + d, 0, rows_total - 1)
        chunks = [pieces[piece_of(row, chunk)].astype(F32) for chunk in range(4)]
        for chunk in range(4):
            for q in range(8):
                shift = (16 - 16 * q) % 128
                near = pltpu.roll(chunks[chunk], shift, 1) if shift else chunks[chunk]
                if q == 0:
                    before = pltpu.roll(chunks[chunk - 1], 16, 1) if chunk else chunks[0]
                    near = jnp.where(lane < 16, before, near)
                if q == 7:
                    after = chunks[chunk + 1] if chunk < 3 else chunks[3]
                    after = pltpu.roll(after, 32 if chunk < 3 else 48, 1)
                    near = jnp.where((lane >= 32) & (lane < 48), after, near)
                at = pl.ds(d * n_frames * 32 + 8 * chunk + q, n_frames, stride=32)
                rolled[at, :] = near
                rolled_far[at, :] = pltpu.roll(near, 64, 1)
        return 0

    lax.fori_loop(0, 5, one_row, 0)

    left = lax.broadcasted_iota(jnp.int32, (32, 128), 1) < 64

    def one_patch(r, _):
        mine = jnp.clip(s - 1 + r, 0, rows_total - 1)
        d = [jnp.clip(mine - 1 + j, 0, rows_total - 1) - (s - 2) for j in range(3)]
        for w in range(8):
            frame = jnp.maximum(2 * t - 6 + w, 0)
            at = [pl.ds(pl.multiple_of((d[j] * n_frames + frame) * 32, 32), 32) for j in range(3)]
            pair = jnp.where(left, rolled[at[0], :], rolled_far[at[1], :])
            patches[r, w, :, :128] = pair.astype(BF16)
            patches[r, w, :, 128:] = rolled[at[2], :].astype(BF16)
        return 0

    lax.fori_loop(0, 3, one_patch, 0)

    def first(r, _):
        lhs = jnp.concatenate([patches[r, i : i + 6].reshape(192, 256) for i in range(3)], axis=1)
        hidden = jnp.dot(lhs, w1[...], preferred_element_type=F32) + b1[...]
        first_act[r] = normed(hidden, g1[...]).reshape(6, 32, 512)
        return 0

    lax.fori_loop(0, 3, first, 0)

    def second(k, _):
        def lhs(rows):
            m = (rows.stop - rows.start) * 128
            return [first_act[rows, i : i + 4].reshape(m, 512) for i in range(3)]

        edge = jnp.dot(
            jnp.concatenate(lhs(slice(0, 2)) + lhs(slice(1, 3)), axis=1),
            jnp.concatenate([w2[i, j, k] for j in (0, 2) for i in range(3)], axis=0),
            preferred_element_type=F32,
        )
        middle = jnp.dot(
            jnp.concatenate(lhs(slice(0, 3)), axis=1),
            jnp.concatenate([w2[i, 1, k] for i in range(3)], axis=0),
            preferred_element_type=F32,
        )
        for p in range(4):
            e, m = p // 2, (p + 1) // 2
            partial[k, p] = edge[e * 128 : (e + 1) * 128] + middle[m * 128 : (m + 1) * 128]
        return 0

    lax.fori_loop(0, 3, second, 0)

    column = lax.broadcasted_iota(jnp.int32, (4, 32, 256), 1)

    def second_norm(p, _):
        a, b, d = [partial[k, p].reshape(4, 32, 256) for k in range(3)]
        a_left = jnp.where(column == 0, a, pltpu.roll(a, 1, 1))
        d_right = jnp.where(column == 31, d, pltpu.roll(d, 31, 1))
        second_act[p, 0] = normed(a_left + b + d + b2[...], g2[...])
        second_act[p, 1] = normed(a + b + d_right + b2[...], g2[...])
        return 0

    lax.fori_loop(0, 4, second_norm, 0)

    def lhs3(rows):
        m = (rows.stop - rows.start) * 128
        return [second_act[rows, :, i : i + 2].reshape(m, 256) for i in range(3)]

    def taps(j):
        return jnp.concatenate(
            [jnp.concatenate([w3[i, j, k] for k in range(3)], axis=1) for i in range(3)], axis=0
        )

    edge = jnp.dot(
        jnp.concatenate(lhs3(slice(0, 3)) + lhs3(slice(1, 4)), axis=1),
        jnp.concatenate([taps(0), taps(2)], axis=0),
        preferred_element_type=F32,
    )
    middle = jnp.dot(
        jnp.concatenate(lhs3(slice(1, 3)), axis=1), taps(1), preferred_element_type=F32
    )
    for r in range(4):
        e, m = (r + 1) // 2, r // 2
        final[r] = edge[e * 128 : (e + 1) * 128] + middle[m * 128 : (m + 1) * 128]

    narrow = lax.broadcasted_iota(jnp.int32, (32, 128), 0)

    def last(r, _):
        def part(q, g, k):
            return final[r, pl.ds((q * 2 + g) * 32, 32), k * 128 : (k + 1) * 128]

        for g in range(2):
            a0, a1, b0, b1_, d0, d1 = [part(q, g, k) for k in range(3) for q in range(2)]
            a_left = jnp.where(narrow == 0, a0, pltpu.roll(a1, 1, 0))
            d_right = jnp.where(narrow == 31, d1, pltpu.roll(d0, 31, 0))
            columns = (a_left + b0 + d0, a0 + b0 + d1, a0 + b1_ + d1, a1 + b1_ + d_right)
            for u, value in enumerate(columns):
                line[g, pl.ds(u, 32, stride=4), :] = value + b3[...]
            out[g, r] = line[g].astype(BF16)
        return 0

    lax.fori_loop(0, 4, last, 0)


def per_device(latent, k1, b1, g1, k2, b2, g2, k3, b3):
    frames, lanes = latent.shape
    tm = lax.axis_size("tm")
    rows_total = lax.axis_size("seq")
    c1, c2, c3 = k1.shape[4], k2.shape[4], k3.shape[4]
    pieces = gathered_pieces(latent)
    w1 = jnp.pad(k1.reshape(3, 3, 48, c1), ((0, 0), (0, 0), (0, 16), (0, 0)))
    w1 = jnp.pad(w1.reshape(3, 192, c1), ((0, 0), (0, 64), (0, 0))).reshape(768, c1)
    vmem = pl.BlockSpec(memory_space=pltpu.VMEM)
    out_frames = frames // tm
    return pl.pallas_call(
        functools.partial(decode_kernel, rows_total),
        out_shape=jax.ShapeDtypeStruct((out_frames, 4, 128, c3), BF16),
        in_specs=[vmem] * 9,
        out_specs=vmem,
        scratch_shapes=[
            pltpu.VMEM((5 * frames * 32, 128), F32),
            pltpu.VMEM((5 * frames * 32, 128), F32),
            pltpu.VMEM((3, 8, 32, 256), BF16),
            pltpu.VMEM((3, 6, 32, c1), BF16),
            pltpu.VMEM((3, 4, 128, c2), F32),
            pltpu.VMEM((4, 2, 4, 32, c2), BF16),
            pltpu.VMEM((4, 128, 3 * c3), F32),
            pltpu.VMEM((2, 128, c3), F32),
        ],
        compiler_params=pltpu.CompilerParams(vmem_limit_bytes=32 * 1024 * 1024),
        cost_estimate=pl.CostEstimate(
            flops=4_000_000_000, bytes_accessed=10_000_000, transcendentals=600_000
        ),
    )(
        pieces,
        w1,
        b1.reshape(1, c1),
        g1.reshape(1, c1),
        pltpu.with_memory_space_constraint(k2, pltpu.VMEM),
        b2.reshape(1, c2),
        g2.reshape(1, c2),
        pltpu.with_memory_space_constraint(k3, pltpu.VMEM),
        b3.reshape(1, c3),
    )


def solution(mesh):
    placed = (P(None, AXES), P(), P(), P(), P(), P(), P(), P(), P())
    return jax.shard_map(
        per_device,
        mesh=mesh,
        in_specs=placed,
        out_specs=P("tm", "seq", None, None),
        check_vma=False,
    )
```

```python
import functools

import jax
import jax.numpy as jnp
from jax import lax
from jax.experimental import pallas as pl
from jax.experimental.pallas import tpu as pltpu
from jax.sharding import PartitionSpec as P

F32, BF16 = jnp.float32, jnp.bfloat16
AXES = ("seq", "tm")


def hop(array, partner, seq, tm):
    pairs = []
    for s in range(seq):
        for t in range(tm):
            s2, t2 = partner(s, t)
            pairs.append((s * tm + t, s2 * tm + t2))
    return lax.ppermute(array, AXES, pairs)


def gathered_pieces(latent):
    seq, tm = lax.axis_size("seq"), lax.axis_size("tm")
    assert seq % 2 == 0 and tm == 4

    def z_partner(first):
        def partner(s, t):
            z = s // 2
            other = z + 1 if (z - first) % 2 == 0 else z - 1
            return (s + 2 * (other - z), t ^ 1) if 0 <= other < seq // 2 else (s, t ^ 1)

        return partner

    beside = hop(latent[None], lambda s, t: (s, t ^ 3), seq, tm)
    own = lax.optimization_barrier(jnp.concatenate([latent[None], jnp.zeros_like(latent)[None]]))
    held = lax.dynamic_update_slice_in_dim(own, beside, 1, 0)
    held = jnp.concatenate([held, hop(held, lambda s, t: (s ^ 1, t ^ 1), seq, tm)])
    even = hop(held, z_partner(0), seq, tm)
    odd = hop(held, z_partner(1), seq, tm)
    held = jnp.concatenate([held, even, odd])
    return held, hop(held, lambda s, t: (s, t ^ 1), seq, tm)


def silu(v):
    return 0.5 * v * (1.0 + jnp.tanh(0.5 * v))


def normed(hidden, gain):
    factor = lax.rsqrt(jnp.mean(hidden * hidden, axis=-1, keepdims=True) + 1e-06)
    return silu(hidden * factor * gain).astype(BF16)


def decode_kernel(
    rows_total,
    held,
    received,
    k1,
    b1_in,
    g1_in,
    k2,
    b2_in,
    g2_in,
    k3,
    b3_in,
    out_hbm,
    pieces,
    rolled,
    rolled_far,
    patches,
    first_act,
    partial,
    second_act,
    final,
    line,
    out,
    w1,
    w2,
    w3,
    b1,
    g1,
    b2,
    g2,
    b3,
    sem1,
    sem2,
    sem3,
    sem_small,
    sem_out,
):
    loads1 = []
    for i in range(3):
        for j in range(3):
            target = w1.at[pl.ds(i * 256 + j * 64, 48)]
            loads1.append(pltpu.make_async_copy(k1.at[i, j], target, sem1.at[i * 3 + j]))
    small = [
        pltpu.make_async_copy(a, b, sem_small.at[n])
        for n, (a, b) in enumerate(
            [(b1_in, b1), (g1_in, g1), (b2_in, b2), (g2_in, g2), (b3_in, b3)]
        )
    ]
    loads2 = [
        pltpu.make_async_copy(k2.at[:, :, k], w2.at[k], sem2.at[k]) for k in range(3)
    ]
    load3 = pltpu.make_async_copy(k3, w3, sem3)
    for copy in loads1 + small + loads2 + [load3]:
        copy.start()
    for i in range(3):
        for start, size in ((48, 16), (112, 16), (176, 80)):
            w1[pl.ds(i * 256 + start, size), :] = jnp.zeros((size, w1.shape[1]), BF16)

    s = lax.axis_index("seq")
    t = lax.axis_index("tm")
    z, x, y, c = s // 2, s % 2, t // 2, t % 2
    n_frames = held.shape[1]
    pieces[:12] = held[...].astype(F32)
    pieces[12:] = received[...].astype(F32)

    def piece_of(row, chunk):
        dz, dx = row // 2 - z, row % 2 ^ x
        dy, dc = chunk // 2 ^ y, chunk % 2 ^ c
        group = jnp.where(dz == 0, 0, jnp.where((dz == 1) == (z % 2 == 0), 1, 2))
        half = (dx + dy + dc + jnp.where(dz == 0, 0, 1)) % 2
        return half * 12 + group * 4 + 2 * dx + dy

    lane = lax.broadcasted_iota(jnp.int32, (n_frames, 128), 1)

    def one_row(d, _):
        row = jnp.clip(s - 2 + d, 0, rows_total - 1)
        chunks = [pieces[piece_of(row, chunk)] for chunk in range(4)]
        for chunk in range(4):
            for q in range(8):
                shift = (16 - 16 * q) % 128
                near = pltpu.roll(chunks[chunk], shift, 1) if shift else chunks[chunk]
                if q == 0:
                    before = pltpu.roll(chunks[chunk - 1], 16, 1) if chunk else chunks[0]
                    near = jnp.where(lane < 16, before, near)
                if q == 7:
                    after = chunks[chunk + 1] if chunk < 3 else chunks[3]
                    after = pltpu.roll(after, 32 if chunk < 3 else 48, 1)
                    near = jnp.where((lane >= 32) & (lane < 48), after, near)
                at = pl.ds(d * n_frames * 32 + 8 * chunk + q, n_frames, stride=32)
                rolled[at, :] = near
                rolled_far[at, :] = pltpu.roll(near, 64, 1)
        return 0

    lax.fori_loop(0, 5, one_row, 0)

    left = lax.broadcasted_iota(jnp.int32, (32, 128), 1) < 64

    def one_patch(r, _):
        mine = jnp.clip(s - 1 + r, 0, rows_total - 1)
        d = [jnp.clip(mine - 1 + j, 0, rows_total - 1) - (s - 2) for j in range(3)]
        for w in range(8):
            frame = jnp.maximum(2 * t - 6 + w, 0)
            at = [pl.ds(pl.multiple_of((d[j] * n_frames + frame) * 32, 32), 32) for j in range(3)]
            pair = jnp.where(left, rolled[at[0], :], rolled_far[at[1], :])
            patches[r, w, :, :128] = pair.astype(BF16)
            patches[r, w, :, 128:] = rolled[at[2], :].astype(BF16)
        return 0

    lax.fori_loop(0, 3, one_patch, 0)

    for copy in loads1 + small:
        copy.wait()

    def first(r, _):
        lhs = jnp.concatenate([patches[r, i : i + 6].reshape(192, 256) for i in range(3)], axis=1)
        hidden = jnp.dot(lhs, w1[...], preferred_element_type=F32) + b1[...]
        first_act[r] = normed(hidden, g1[...]).reshape(6, 32, 512)
        return 0

    lax.fori_loop(0, 3, first, 0)

    def second(k, _):
        pltpu.make_async_copy(k2.at[:, :, k], w2.at[k], sem2.at[k]).wait()

        def lhs(rows):
            m = (rows.stop - rows.start) * 128
            return [first_act[rows, i : i + 4].reshape(m, 512) for i in range(3)]

        edge = jnp.dot(
            jnp.concatenate(lhs(slice(0, 2)) + lhs(slice(1, 3)), axis=1),
            jnp.concatenate([w2[k, i, j] for j in (0, 2) for i in range(3)], axis=0),
            preferred_element_type=F32,
        )
        middle = jnp.dot(
            jnp.concatenate(lhs(slice(0, 3)), axis=1),
            jnp.concatenate([w2[k, i, 1] for i in range(3)], axis=0),
            preferred_element_type=F32,
        )
        for p in range(4):
            e, m = p // 2, (p + 1) // 2
            partial[k, p] = edge[e * 128 : (e + 1) * 128] + middle[m * 128 : (m + 1) * 128]
        return 0

    lax.fori_loop(0, 3, second, 0)

    column = lax.broadcasted_iota(jnp.int32, (4, 32, 256), 1)

    def second_norm(p, _):
        a, b, d = [partial[k, p].reshape(4, 32, 256) for k in range(3)]
        a_left = jnp.where(column == 0, a, pltpu.roll(a, 1, 1))
        d_right = jnp.where(column == 31, d, pltpu.roll(d, 31, 1))
        second_act[p, 0] = normed(a_left + b + d + b2[...], g2[...])
        second_act[p, 1] = normed(a + b + d_right + b2[...], g2[...])
        return 0

    lax.fori_loop(0, 4, second_norm, 0)

    load3.wait()

    def lhs3(rows):
        m = (rows.stop - rows.start) * 128
        return [second_act[rows, :, i : i + 2].reshape(m, 256) for i in range(3)]

    def taps(j):
        return jnp.concatenate(
            [jnp.concatenate([w3[i, j, k] for k in range(3)], axis=1) for i in range(3)], axis=0
        )

    edge = jnp.dot(
        jnp.concatenate(lhs3(slice(0, 3)) + lhs3(slice(1, 4)), axis=1),
        jnp.concatenate([taps(0), taps(2)], axis=0),
        preferred_element_type=F32,
    )
    middle = jnp.dot(
        jnp.concatenate(lhs3(slice(1, 3)), axis=1), taps(1), preferred_element_type=F32
    )
    for r in range(4):
        e, m = (r + 1) // 2, r // 2
        final[r] = edge[e * 128 : (e + 1) * 128] + middle[m * 128 : (m + 1) * 128]

    narrow = lax.broadcasted_iota(jnp.int32, (32, 128), 0)

    def last(r, _):
        def part(q, g, k):
            return final[r, pl.ds((q * 2 + g) * 32, 32), k * 128 : (k + 1) * 128]

        for g in range(2):
            a0, a1, b0, b1_, d0, d1 = [part(q, g, k) for k in range(3) for q in range(2)]
            a_left = jnp.where(narrow == 0, a0, pltpu.roll(a1, 1, 0))
            d_right = jnp.where(narrow == 31, d1, pltpu.roll(d0, 31, 0))
            columns = (a_left + b0 + d0, a0 + b0 + d1, a0 + b1_ + d1, a1 + b1_ + d_right)
            for u, value in enumerate(columns):
                line[g, pl.ds(u, 32, stride=4), :] = value + b3[...]
            out[g, r] = line[g].astype(BF16)
        pltpu.make_async_copy(out.at[:, r], out_hbm.at[:, r], sem_out.at[r]).start()
        return 0

    lax.fori_loop(0, 4, last, 0)
    for r in range(4):
        pltpu.make_async_copy(out.at[:, r], out_hbm.at[:, r], sem_out.at[r]).wait()


def per_device(latent, k1, b1, g1, k2, b2, g2, k3, b3):
    frames, lanes = latent.shape
    tm = lax.axis_size("tm")
    rows_total = lax.axis_size("seq")
    c1, c2, c3 = k1.shape[4], k2.shape[4], k3.shape[4]
    held, received = gathered_pieces(latent)
    vmem = pl.BlockSpec(memory_space=pltpu.VMEM)
    hbm = pl.BlockSpec(memory_space=pltpu.HBM)
    out_frames = frames // tm
    return pl.pallas_call(
        functools.partial(decode_kernel, rows_total),
        out_shape=jax.ShapeDtypeStruct((out_frames, 4, 128, c3), BF16),
        in_specs=[vmem] * 2 + [hbm] * 8,
        out_specs=hbm,
        scratch_shapes=[
            pltpu.VMEM((24, frames, 128), F32),
            pltpu.VMEM((5 * frames * 32, 128), F32),
            pltpu.VMEM((5 * frames * 32, 128), F32),
            pltpu.VMEM((3, 8, 32, 256), BF16),
            pltpu.VMEM((3, 6, 32, c1), BF16),
            pltpu.VMEM((3, 4, 128, c2), F32),
            pltpu.VMEM((4, 2, 4, 32, c2), BF16),
            pltpu.VMEM((4, 128, 3 * c3), F32),
            pltpu.VMEM((2, 128, c3), F32),
            pltpu.VMEM((out_frames, 4, 128, c3), BF16),
            pltpu.VMEM((768, c1), BF16),
            pltpu.VMEM((3, 3, 3, c1, c2), BF16),
            pltpu.VMEM((3, 3, 3, c2, c3), BF16),
            pltpu.VMEM((1, c1), F32),
            pltpu.VMEM((1, c1), F32),
            pltpu.VMEM((1, c2), F32),
            pltpu.VMEM((1, c2), F32),
            pltpu.VMEM((1, c3), F32),
            pltpu.SemaphoreType.DMA((9,)),
            pltpu.SemaphoreType.DMA((3,)),
            pltpu.SemaphoreType.DMA,
            pltpu.SemaphoreType.DMA((5,)),
            pltpu.SemaphoreType.DMA((4,)),
        ],
        compiler_params=pltpu.CompilerParams(vmem_limit_bytes=32 * 1024 * 1024),
        cost_estimate=pl.CostEstimate(
            flops=4_000_000_000, bytes_accessed=10_000_000, transcendentals=600_000
        ),
    )(
        held,
        received,
        *[
            pltpu.with_memory_space_constraint(array, pltpu.HBM)
            for array in (
                k1.reshape(3, 3, 48, c1),
                b1.reshape(1, c1),
                g1.reshape(1, c1),
                k2,
                b2.reshape(1, c2),
                g2.reshape(1, c2),
                k3,
                b3.reshape(1, c3),
            )
        ],
    )


def solution(mesh):
    placed = (P(None, AXES), P(), P(), P(), P(), P(), P(), P(), P())
    return jax.shard_map(
        per_device,
        mesh=mesh,
        in_specs=placed,
        out_specs=P("tm", "seq", None, None),
        check_vma=False,
    )
```

```python
import functools

import jax
import jax.numpy as jnp
from jax import lax
from jax.experimental import pallas as pl
from jax.experimental.pallas import tpu as pltpu
from jax.sharding import PartitionSpec as P

F32, BF16 = jnp.float32, jnp.bfloat16
AXES = ("seq", "tm")


def hop(array, partner, seq, tm):
    pairs = []
    for s in range(seq):
        for t in range(tm):
            s2, t2 = partner(s, t)
            pairs.append((s * tm + t, s2 * tm + t2))
    return lax.ppermute(array, AXES, pairs)


def gathered_pieces(latent, k1, b1, g1, k2, b2, g2, b3):
    seq, tm = lax.axis_size("seq"), lax.axis_size("tm")
    assert seq % 2 == 0 and tm == 4

    def z_partner(first):
        def partner(s, t):
            z = s // 2
            other = z + 1 if (z - first) % 2 == 0 else z - 1
            return (s + 2 * (other - z), t ^ 1) if 0 <= other < seq // 2 else (s, t ^ 1)

        return partner

    beside = hop(latent[None], lambda s, t: (s, t ^ 3), seq, tm)
    tap0, own = fetched_tap_and_latent(k2, 0, latent)
    beside, tap0, own = lax.optimization_barrier((beside, tap0, own))
    held = jnp.concatenate([own, beside])

    k2, _ = lax.optimization_barrier((k2, beside))
    across = hop(held, lambda s, t: (s ^ 1, t ^ 1), seq, tm)
    tap1 = fetched_tap(k2, 1)
    across, tap1 = lax.optimization_barrier((across, tap1))
    held = jnp.concatenate([held, across])

    k2, _ = lax.optimization_barrier((k2, across))
    even = hop(held, z_partner(0), seq, tm)
    odd = hop(held, z_partner(1), seq, tm)
    tap2 = fetched_tap(k2, 2)
    even, odd, tap2 = lax.optimization_barrier((even, odd, tap2))
    held = jnp.concatenate([held, even, odd])

    k1, _ = lax.optimization_barrier((k1, even))
    received = hop(held, lambda s, t: (s, t ^ 1), seq, tm)
    first = fetched_first(k1, b1, g1, b2, g2, b3)
    return held, received, first, (tap0, tap1, tap2)


def normed(hidden, gain):
    factor = lax.rsqrt(jnp.mean(hidden * hidden, axis=-1, keepdims=True) + 1e-06)
    half = hidden * (0.5 * factor) * gain
    return (half + half * jnp.tanh(half)).astype(BF16)


def first_weights_kernel(k1, b1_in, g1_in, b2_in, g2_in, b3_in, w1, b1, g1, b2, g2, b3, sem):
    pairs = [(b1_in, b1), (g1_in, g1), (b2_in, b2), (g2_in, g2), (b3_in, b3)]
    for i in range(3):
        for j in range(3):
            pairs.append((k1.at[i, j], w1.at[pl.ds(i * 256 + j * 64, 48)]))
    copies = [pltpu.make_async_copy(a, b, sem.at[n]) for n, (a, b) in enumerate(pairs)]
    for copy in copies:
        copy.start()
    for i in range(3):
        for start, size in ((48, 16), (112, 16), (176, 80)):
            w1[pl.ds(i * 256 + start, size), :] = jnp.zeros((size, w1.shape[1]), BF16)
    for copy in copies:
        copy.wait()


def column_tap_kernel(k, k2, w2, sem):
    copy = pltpu.make_async_copy(k2.at[:, :, k], w2, sem)
    copy.start()
    copy.wait()


def column_tap_and_latent_kernel(k, k2, latent, w2, own, sem):
    copies = [
        pltpu.make_async_copy(latent, own.at[0], sem.at[0]),
        pltpu.make_async_copy(k2.at[:, :, k], w2, sem.at[1]),
    ]
    for copy in copies:
        copy.start()
    for copy in copies:
        copy.wait()


def in_hbm(*arrays):
    return [pltpu.with_memory_space_constraint(array, pltpu.HBM) for array in arrays]


def fetched_first(k1, b1, g1, b2, g2, b3):
    c1 = k1.shape[4]
    shapes = [(768, c1)] + [(1, v.shape[0]) for v in (b1, g1, b2, g2, b3)]
    rows = [v.reshape(1, -1) for v in (b1, g1, b2, g2, b3)]
    return pl.pallas_call(
        first_weights_kernel,
        out_shape=[pltpu.VMEM(shapes[0], BF16)] + [pltpu.VMEM(v, F32) for v in shapes[1:]],
        in_specs=[pl.BlockSpec(memory_space=pltpu.HBM)] * 6,
        out_specs=[pl.BlockSpec(memory_space=pltpu.VMEM)] * 6,
        scratch_shapes=[pltpu.SemaphoreType.DMA((14,))],
        cost_estimate=pl.CostEstimate(flops=0, bytes_accessed=3_000_000, transcendentals=0),
    )(*in_hbm(k1.reshape(3, 3, 48, c1), *rows))


def fetched_tap(k2, k):
    shape = k2.shape[:2] + k2.shape[3:]
    return pl.pallas_call(
        functools.partial(column_tap_kernel, k),
        out_shape=pltpu.VMEM(shape, BF16),
        in_specs=[pl.BlockSpec(memory_space=pltpu.HBM)],
        out_specs=pl.BlockSpec(memory_space=pltpu.VMEM),
        scratch_shapes=[pltpu.SemaphoreType.DMA],
        cost_estimate=pl.CostEstimate(flops=0, bytes_accessed=4_500_000, transcendentals=0),
    )(*in_hbm(k2))


def fetched_tap_and_latent(k2, k, latent):
    shape = k2.shape[:2] + k2.shape[3:]
    return pl.pallas_call(
        functools.partial(column_tap_and_latent_kernel, k),
        out_shape=[pltpu.VMEM(shape, BF16), pltpu.VMEM((1,) + latent.shape, BF16)],
        in_specs=[pl.BlockSpec(memory_space=pltpu.HBM)] * 2,
        out_specs=[pl.BlockSpec(memory_space=pltpu.VMEM)] * 2,
        scratch_shapes=[pltpu.SemaphoreType.DMA((2,))],
        cost_estimate=pl.CostEstimate(flops=0, bytes_accessed=4_500_000, transcendentals=0),
    )(*in_hbm(k2, latent))


def decode_kernel(
    rows_total,
    held,
    received,
    w1,
    b1,
    g1,
    b2,
    g2,
    b3,
    w2_0,
    w2_1,
    w2_2,
    k3,
    out_hbm,
    pieces,
    rolled,
    rolled_far,
    patches,
    first_act,
    partial,
    second_act,
    final,
    line,
    out,
    w3,
    sem3,
    sem_out,
):
    load3 = pltpu.make_async_copy(k3, w3, sem3)
    load3.start()
    s = lax.axis_index("seq")
    t = lax.axis_index("tm")
    z, x, y, c = s // 2, s % 2, t // 2, t % 2
    n_frames = held.shape[1]
    pieces[:12] = held[...].astype(F32)
    pieces[12:] = received[...].astype(F32)

    def piece_of(row, chunk):
        dz, dx = row // 2 - z, row % 2 ^ x
        dy, dc = chunk // 2 ^ y, chunk % 2 ^ c
        group = jnp.where(dz == 0, 0, jnp.where((dz == 1) == (z % 2 == 0), 1, 2))
        half = (dx + dy + dc + jnp.where(dz == 0, 0, 1)) % 2
        return half * 12 + group * 4 + 2 * dx + dy

    lane = lax.broadcasted_iota(jnp.int32, (n_frames, 128), 1)

    def one_row(d, _):
        row = jnp.clip(s - 2 + d, 0, rows_total - 1)
        chunks = [pieces[piece_of(row, chunk)] for chunk in range(4)]
        for chunk in range(4):
            for q in range(8):
                shift = (16 - 16 * q) % 128
                near = pltpu.roll(chunks[chunk], shift, 1) if shift else chunks[chunk]
                if q == 0:
                    before = pltpu.roll(chunks[chunk - 1], 16, 1) if chunk else chunks[0]
                    near = jnp.where(lane < 16, before, near)
                if q == 7:
                    after = chunks[chunk + 1] if chunk < 3 else chunks[3]
                    after = pltpu.roll(after, 32 if chunk < 3 else 48, 1)
                    near = jnp.where((lane >= 32) & (lane < 48), after, near)
                at = pl.ds(d * n_frames * 32 + 8 * chunk + q, n_frames, stride=32)
                rolled[at, :] = near
                rolled_far[at, :] = pltpu.roll(near, 64, 1)
        return 0

    lax.fori_loop(0, 5, one_row, 0)

    left = lax.broadcasted_iota(jnp.int32, (32, 128), 1) < 64

    def one_patch(r, _):
        mine = jnp.clip(s - 1 + r, 0, rows_total - 1)
        d = [jnp.clip(mine - 1 + j, 0, rows_total - 1) - (s - 2) for j in range(3)]
        for w in range(8):
            frame = jnp.maximum(2 * t - 6 + w, 0)
            at = [pl.ds(pl.multiple_of((d[j] * n_frames + frame) * 32, 32), 32) for j in range(3)]
            pair = jnp.where(left, rolled[at[0], :], rolled_far[at[1], :])
            patches[r, w, :, :128] = pair.astype(BF16)
            patches[r, w, :, 128:] = rolled[at[2], :].astype(BF16)
        return 0

    lax.fori_loop(0, 3, one_patch, 0)

    def first(r):
        lhs = jnp.concatenate([patches[r, i : i + 6].reshape(192, 256) for i in range(3)], axis=1)
        hidden = jnp.dot(lhs, w1[...], preferred_element_type=F32) + b1[...]
        first_act[r] = normed(hidden, g1[...]).reshape(6, 32, 512)

    for r in range(3):
        first(r)

    def second(k, w2):
        def lhs(rows):
            m = (rows.stop - rows.start) * 128
            return [first_act[rows, i : i + 4].reshape(m, 512) for i in range(3)]

        edge = jnp.dot(
            jnp.concatenate(lhs(slice(0, 2)) + lhs(slice(1, 3)), axis=1),
            jnp.concatenate([w2[i, j] for j in (0, 2) for i in range(3)], axis=0),
            preferred_element_type=F32,
        )
        middle = jnp.dot(
            jnp.concatenate(lhs(slice(0, 3)), axis=1),
            jnp.concatenate([w2[i, 1] for i in range(3)], axis=0),
            preferred_element_type=F32,
        )
        for p in range(4):
            e, m = p // 2, (p + 1) // 2
            partial[k, p] = edge[e * 128 : (e + 1) * 128] + middle[m * 128 : (m + 1) * 128]

    for k, w2 in enumerate((w2_0, w2_1, w2_2)):
        second(k, w2)

    column = lax.broadcasted_iota(jnp.int32, (4, 32, 256), 1)

    def second_norm(p):
        a, b, d = [partial[k, p].reshape(4, 32, 256) for k in range(3)]
        a_left = jnp.where(column == 0, a, pltpu.roll(a, 1, 1))
        d_right = jnp.where(column == 31, d, pltpu.roll(d, 31, 1))
        second_act[p, 0] = normed(a_left + b + d + b2[...], g2[...])
        second_act[p, 1] = normed(a + b + d_right + b2[...], g2[...])

    for p in range(4):
        second_norm(p)

    load3.wait()

    def lhs3(rows):
        m = (rows.stop - rows.start) * 128
        return [second_act[rows, :, i : i + 2].reshape(m, 256) for i in range(3)]

    def taps(j):
        return jnp.concatenate(
            [jnp.concatenate([w3[i, j, k] for k in range(3)], axis=1) for i in range(3)], axis=0
        )

    edge = jnp.dot(
        jnp.concatenate(lhs3(slice(0, 3)) + lhs3(slice(1, 4)), axis=1),
        jnp.concatenate([taps(0), taps(2)], axis=0),
        preferred_element_type=F32,
    )
    middle = jnp.dot(
        jnp.concatenate(lhs3(slice(1, 3)), axis=1), taps(1), preferred_element_type=F32
    )
    for r in range(4):
        e, m = (r + 1) // 2, r // 2
        final[r] = edge[e * 128 : (e + 1) * 128] + middle[m * 128 : (m + 1) * 128]

    narrow = lax.broadcasted_iota(jnp.int32, (32, 128), 0)

    def last(r):
        def part(q, g, k):
            return final[r, pl.ds((q * 2 + g) * 32, 32), k * 128 : (k + 1) * 128]

        for g in range(2):
            a0, a1, b0, b1_, d0, d1 = [part(q, g, k) for k in range(3) for q in range(2)]
            a_left = jnp.where(narrow == 0, a0, pltpu.roll(a1, 1, 0))
            d_right = jnp.where(narrow == 31, d1, pltpu.roll(d0, 31, 0))
            columns = (a_left + b0 + d0, a0 + b0 + d1, a0 + b1_ + d1, a1 + b1_ + d_right)
            for u, value in enumerate(columns):
                line[g, pl.ds(u, 32, stride=4), :] = value + b3[...]
            out[g, r] = line[g].astype(BF16)
        pltpu.make_async_copy(out.at[:, r], out_hbm.at[:, r], sem_out.at[r]).start()

    for r in range(4):
        last(r)
    for r in range(4):
        pltpu.make_async_copy(out.at[:, r], out_hbm.at[:, r], sem_out.at[r]).wait()


def per_device(latent, k1, b1, g1, k2, b2, g2, k3, b3):
    frames, lanes = latent.shape
    tm = lax.axis_size("tm")
    rows_total = lax.axis_size("seq")
    c1, c2, c3 = k1.shape[4], k2.shape[4], k3.shape[4]
    held, received, first, taps = gathered_pieces(latent, k1, b1, g1, k2, b2, g2, b3)
    vmem = pl.BlockSpec(memory_space=pltpu.VMEM)
    hbm = pl.BlockSpec(memory_space=pltpu.HBM)
    out_frames = frames // tm
    return pl.pallas_call(
        functools.partial(decode_kernel, rows_total),
        out_shape=jax.ShapeDtypeStruct((out_frames, 4, 128, c3), BF16),
        in_specs=[vmem] * 11 + [hbm],
        out_specs=hbm,
        scratch_shapes=[
            pltpu.VMEM((24, frames, 128), F32),
            pltpu.VMEM((5 * frames * 32, 128), F32),
            pltpu.VMEM((5 * frames * 32, 128), F32),
            pltpu.VMEM((3, 8, 32, 256), BF16),
            pltpu.VMEM((3, 6, 32, c1), BF16),
            pltpu.VMEM((3, 4, 128, c2), F32),
            pltpu.VMEM((4, 2, 4, 32, c2), BF16),
            pltpu.VMEM((4, 128, 3 * c3), F32),
            pltpu.VMEM((2, 128, c3), F32),
            pltpu.VMEM((out_frames, 4, 128, c3), BF16),
            pltpu.VMEM((3, 3, 3, c2, c3), BF16),
            pltpu.SemaphoreType.DMA,
            pltpu.SemaphoreType.DMA((4,)),
        ],
        compiler_params=pltpu.CompilerParams(vmem_limit_bytes=24 * 1024 * 1024),
        cost_estimate=pl.CostEstimate(
            flops=4_000_000_000, bytes_accessed=10_000_000, transcendentals=600_000
        ),
    )(held, received, *first, *taps, *in_hbm(k3))


def solution(mesh):
    placed = (P(None, AXES), P(), P(), P(), P(), P(), P(), P(), P())
    return jax.shard_map(
        per_device,
        mesh=mesh,
        in_specs=placed,
        out_specs=P("tm", "seq", None, None),
        check_vma=False,
    )
```

```python
import functools

import jax
import jax.numpy as jnp
from jax import lax
from jax.experimental import pallas as pl
from jax.experimental.pallas import tpu as pltpu
from jax.sharding import PartitionSpec as P

F32, BF16 = jnp.float32, jnp.bfloat16
AXES = ("seq", "tm")


def hop(array, partner, seq, tm):
    pairs = []
    for s in range(seq):
        for t in range(tm):
            s2, t2 = partner(s, t)
            pairs.append((s * tm + t, s2 * tm + t2))
    return lax.ppermute(array, AXES, pairs)


def gathered_pieces(latent, k1, b1, g1, k2, b2, g2, b3):
    seq, tm = lax.axis_size("seq"), lax.axis_size("tm")
    assert seq % 2 == 0 and tm == 4

    def z_partner(first):
        def partner(s, t):
            z = s // 2
            other = z + 1 if (z - first) % 2 == 0 else z - 1
            return (s + 2 * (other - z), t ^ 1) if 0 <= other < seq // 2 else (s, t ^ 1)

        return partner

    beside = hop(latent[None], lambda s, t: (s, t ^ 3), seq, tm)
    tap0, own = fetched_tap_and_latent(k2, 0, latent)
    beside, tap0, own = lax.optimization_barrier((beside, tap0, own))
    held = jnp.concatenate([own, beside])

    k2, _ = lax.optimization_barrier((k2, beside))
    across = hop(held, lambda s, t: (s ^ 1, t ^ 1), seq, tm)
    tap1 = fetched_tap(k2, 1)
    across, tap1 = lax.optimization_barrier((across, tap1))
    held = jnp.concatenate([held, across])

    k2, _ = lax.optimization_barrier((k2, across))
    even = hop(held, z_partner(0), seq, tm)
    odd = hop(held, z_partner(1), seq, tm)
    tap2 = fetched_tap(k2, 2)
    even, odd, tap2 = lax.optimization_barrier((even, odd, tap2))
    held = jnp.concatenate([held, even, odd])

    k1, _ = lax.optimization_barrier((k1, even))
    received = hop(held, lambda s, t: (s, t ^ 1), seq, tm)
    first = fetched_first(k1, b1, g1, b2, g2, b3)
    return held, received, first, (tap0, tap1, tap2)


def normed(hidden, gain):
    factor = lax.rsqrt(jnp.mean(hidden * hidden, axis=-1, keepdims=True) + 1e-06)
    half = hidden * (0.5 * factor) * gain
    return (half + half * jnp.tanh(half)).astype(BF16)


def first_weights_kernel(k1, b1_in, g1_in, b2_in, g2_in, b3_in, w1, b1, g1, b2, g2, b3, sem):
    pairs = [(b1_in, b1), (g1_in, g1), (b2_in, b2), (g2_in, g2), (b3_in, b3)]
    for i in range(3):
        for j in range(3):
            pairs.append((k1.at[i, j], w1.at[pl.ds(i * 256 + j * 64, 48)]))
    copies = [pltpu.make_async_copy(a, b, sem.at[n]) for n, (a, b) in enumerate(pairs)]
    for copy in copies:
        copy.start()
    for i in range(3):
        for start, size in ((48, 16), (112, 16), (176, 80)):
            w1[pl.ds(i * 256 + start, size), :] = jnp.zeros((size, w1.shape[1]), BF16)
    for copy in copies:
        copy.wait()


def column_tap_kernel(k, k2, w2, sem):
    copy = pltpu.make_async_copy(k2.at[:, :, k], w2, sem)
    copy.start()
    copy.wait()


def column_tap_and_latent_kernel(k, k2, latent, w2, own, sem):
    copies = [
        pltpu.make_async_copy(latent, own.at[0], sem.at[0]),
        pltpu.make_async_copy(k2.at[:, :, k], w2, sem.at[1]),
    ]
    for copy in copies:
        copy.start()
    for copy in copies:
        copy.wait()


def in_hbm(*arrays):
    return [pltpu.with_memory_space_constraint(array, pltpu.HBM) for array in arrays]


def fetched_first(k1, b1, g1, b2, g2, b3):
    c1 = k1.shape[4]
    shapes = [(768, c1)] + [(1, v.shape[0]) for v in (b1, g1, b2, g2, b3)]
    rows = [v.reshape(1, -1) for v in (b1, g1, b2, g2, b3)]
    return pl.pallas_call(
        first_weights_kernel,
        out_shape=[pltpu.VMEM(shapes[0], BF16)] + [pltpu.VMEM(v, F32) for v in shapes[1:]],
        in_specs=[pl.BlockSpec(memory_space=pltpu.HBM)] * 6,
        out_specs=[pl.BlockSpec(memory_space=pltpu.VMEM)] * 6,
        scratch_shapes=[pltpu.SemaphoreType.DMA((14,))],
        compiler_params=pltpu.CompilerParams(vmem_limit_bytes=1024 * 1024),
        cost_estimate=pl.CostEstimate(flops=0, bytes_accessed=3_000_000, transcendentals=0),
    )(*in_hbm(k1.reshape(3, 3, 48, c1), *rows))


def fetched_tap(k2, k):
    shape = k2.shape[:2] + k2.shape[3:]
    return pl.pallas_call(
        functools.partial(column_tap_kernel, k),
        out_shape=pltpu.VMEM(shape, BF16),
        in_specs=[pl.BlockSpec(memory_space=pltpu.HBM)],
        out_specs=pl.BlockSpec(memory_space=pltpu.VMEM),
        scratch_shapes=[pltpu.SemaphoreType.DMA],
        compiler_params=pltpu.CompilerParams(vmem_limit_bytes=1024 * 1024),
        cost_estimate=pl.CostEstimate(flops=0, bytes_accessed=4_500_000, transcendentals=0),
    )(*in_hbm(k2))


def fetched_tap_and_latent(k2, k, latent):
    shape = k2.shape[:2] + k2.shape[3:]
    return pl.pallas_call(
        functools.partial(column_tap_and_latent_kernel, k),
        out_shape=[pltpu.VMEM(shape, BF16), pltpu.VMEM((1,) + latent.shape, BF16)],
        in_specs=[pl.BlockSpec(memory_space=pltpu.HBM)] * 2,
        out_specs=[pl.BlockSpec(memory_space=pltpu.VMEM)] * 2,
        scratch_shapes=[pltpu.SemaphoreType.DMA((2,))],
        compiler_params=pltpu.CompilerParams(vmem_limit_bytes=1024 * 1024),
        cost_estimate=pl.CostEstimate(flops=0, bytes_accessed=4_500_000, transcendentals=0),
    )(*in_hbm(k2, latent))


def decode_kernel(
    rows_total,
    held,
    received,
    w1,
    b1,
    g1,
    b2,
    g2,
    b3,
    w2_0,
    w2_1,
    w2_2,
    k3,
    out_hbm,
    pieces,
    rolled,
    rolled_far,
    patches,
    first_act,
    partial,
    second_act,
    final,
    line,
    out,
    w3,
    sem3,
    sem_out,
):
    load3 = pltpu.make_async_copy(k3, w3, sem3)
    load3.start()
    s = lax.axis_index("seq")
    t = lax.axis_index("tm")
    z, x, y, c = s // 2, s % 2, t // 2, t % 2
    n_frames = held.shape[1]
    pieces[:12] = held[...].astype(F32)
    pieces[12:] = received[...].astype(F32)

    def piece_of(row, chunk):
        dz, dx = row // 2 - z, row % 2 ^ x
        dy, dc = chunk // 2 ^ y, chunk % 2 ^ c
        group = jnp.where(dz == 0, 0, jnp.where((dz == 1) == (z % 2 == 0), 1, 2))
        half = (dx + dy + dc + jnp.where(dz == 0, 0, 1)) % 2
        return half * 12 + group * 4 + 2 * dx + dy

    lane = lax.broadcasted_iota(jnp.int32, (n_frames, 128), 1)

    def one_row(d, _):
        row = jnp.clip(s - 2 + d, 0, rows_total - 1)
        chunks = [pieces[piece_of(row, chunk)] for chunk in range(4)]
        for chunk in range(4):
            for q in range(8):
                shift = (16 - 16 * q) % 128
                near = pltpu.roll(chunks[chunk], shift, 1) if shift else chunks[chunk]
                if q == 0:
                    before = pltpu.roll(chunks[chunk - 1], 16, 1) if chunk else chunks[0]
                    near = jnp.where(lane < 16, before, near)
                if q == 7:
                    after = chunks[chunk + 1] if chunk < 3 else chunks[3]
                    after = pltpu.roll(after, 32 if chunk < 3 else 48, 1)
                    near = jnp.where((lane >= 32) & (lane < 48), after, near)
                at = pl.ds(d * n_frames * 32 + 8 * chunk + q, n_frames, stride=32)
                rolled[at, :] = near
                rolled_far[at, :] = pltpu.roll(near, 64, 1)
        return 0

    lax.fori_loop(0, 5, one_row, 0)

    left = lax.broadcasted_iota(jnp.int32, (32, 128), 1) < 64

    def one_patch(r, _):
        mine = jnp.clip(s - 1 + r, 0, rows_total - 1)
        d = [jnp.clip(mine - 1 + j, 0, rows_total - 1) - (s - 2) for j in range(3)]
        for w in range(8):
            frame = jnp.maximum(2 * t - 6 + w, 0)
            at = [pl.ds(pl.multiple_of((d[j] * n_frames + frame) * 32, 32), 32) for j in range(3)]
            pair = jnp.where(left, rolled[at[0], :], rolled_far[at[1], :])
            patches[r, w, :, :128] = pair.astype(BF16)
            patches[r, w, :, 128:] = rolled[at[2], :].astype(BF16)
        return 0

    lax.fori_loop(0, 3, one_patch, 0)

    def first(r):
        lhs = jnp.concatenate([patches[r, i : i + 6].reshape(192, 256) for i in range(3)], axis=1)
        hidden = jnp.dot(lhs, w1[...], preferred_element_type=F32) + b1[...]
        first_act[r] = normed(hidden, g1[...]).reshape(6, 32, 512)

    for r in range(3):
        first(r)

    def second(k, w2):
        def lhs(rows):
            m = (rows.stop - rows.start) * 128
            return [first_act[rows, i : i + 4].reshape(m, 512) for i in range(3)]

        edge = jnp.dot(
            jnp.concatenate(lhs(slice(0, 2)) + lhs(slice(1, 3)), axis=1),
            jnp.concatenate([w2[i, j] for j in (0, 2) for i in range(3)], axis=0),
            preferred_element_type=F32,
        )
        middle = jnp.dot(
            jnp.concatenate(lhs(slice(0, 3)), axis=1),
            jnp.concatenate([w2[i, 1] for i in range(3)], axis=0),
            preferred_element_type=F32,
        )
        for p in range(4):
            e, m = p // 2, (p + 1) // 2
            partial[k, p] = edge[e * 128 : (e + 1) * 128] + middle[m * 128 : (m + 1) * 128]

    for k, w2 in enumerate((w2_0, w2_1, w2_2)):
        second(k, w2)

    column = lax.broadcasted_iota(jnp.int32, (4, 32, 256), 1)

    def second_norm(p):
        a, b, d = [partial[k, p].reshape(4, 32, 256) for k in range(3)]
        a_left = jnp.where(column == 0, a, pltpu.roll(a, 1, 1))
        d_right = jnp.where(column == 31, d, pltpu.roll(d, 31, 1))
        second_act[p, 0] = normed(a_left + b + d + b2[...], g2[...])
        second_act[p, 1] = normed(a + b + d_right + b2[...], g2[...])

    for p in range(4):
        second_norm(p)

    load3.wait()

    def lhs3(rows):
        m = (rows.stop - rows.start) * 128
        return [second_act[rows, :, i : i + 2].reshape(m, 256) for i in range(3)]

    def taps(j):
        return jnp.concatenate(
            [jnp.concatenate([w3[i, j, k] for k in range(3)], axis=1) for i in range(3)], axis=0
        )

    edge = jnp.dot(
        jnp.concatenate(lhs3(slice(0, 3)) + lhs3(slice(1, 4)), axis=1),
        jnp.concatenate([taps(0), taps(2)], axis=0),
        preferred_element_type=F32,
    )
    middle = jnp.dot(
        jnp.concatenate(lhs3(slice(1, 3)), axis=1), taps(1), preferred_element_type=F32
    )
    for r in range(4):
        e, m = (r + 1) // 2, r // 2
        final[r] = edge[e * 128 : (e + 1) * 128] + middle[m * 128 : (m + 1) * 128]

    narrow = lax.broadcasted_iota(jnp.int32, (32, 128), 0)

    def last(r):
        def part(q, g, k):
            return final[r, pl.ds((q * 2 + g) * 32, 32), k * 128 : (k + 1) * 128]

        for g in range(2):
            a0, a1, b0, b1_, d0, d1 = [part(q, g, k) for k in range(3) for q in range(2)]
            a_left = jnp.where(narrow == 0, a0, pltpu.roll(a1, 1, 0))
            d_right = jnp.where(narrow == 31, d1, pltpu.roll(d0, 31, 0))
            columns = (a_left + b0 + d0, a0 + b0 + d1, a0 + b1_ + d1, a1 + b1_ + d_right)
            for u, value in enumerate(columns):
                line[g, pl.ds(u, 32, stride=4), :] = value + b3[...]
            out[g, r] = line[g].astype(BF16)
        pltpu.make_async_copy(out.at[:, r], out_hbm.at[:, r], sem_out.at[r]).start()

    for r in range(4):
        last(r)
    for r in range(4):
        pltpu.make_async_copy(out.at[:, r], out_hbm.at[:, r], sem_out.at[r]).wait()


def per_device(latent, k1, b1, g1, k2, b2, g2, k3, b3):
    frames, lanes = latent.shape
    tm = lax.axis_size("tm")
    rows_total = lax.axis_size("seq")
    c1, c2, c3 = k1.shape[4], k2.shape[4], k3.shape[4]
    held, received, first, taps = gathered_pieces(latent, k1, b1, g1, k2, b2, g2, b3)
    vmem = pl.BlockSpec(memory_space=pltpu.VMEM)
    hbm = pl.BlockSpec(memory_space=pltpu.HBM)
    out_frames = frames // tm
    return pl.pallas_call(
        functools.partial(decode_kernel, rows_total),
        out_shape=jax.ShapeDtypeStruct((out_frames, 4, 128, c3), BF16),
        in_specs=[vmem] * 11 + [hbm],
        out_specs=hbm,
        scratch_shapes=[
            pltpu.VMEM((24, frames, 128), F32),
            pltpu.VMEM((5 * frames * 32, 128), F32),
            pltpu.VMEM((5 * frames * 32, 128), F32),
            pltpu.VMEM((3, 8, 32, 256), BF16),
            pltpu.VMEM((3, 6, 32, c1), BF16),
            pltpu.VMEM((3, 4, 128, c2), F32),
            pltpu.VMEM((4, 2, 4, 32, c2), BF16),
            pltpu.VMEM((4, 128, 3 * c3), F32),
            pltpu.VMEM((2, 128, c3), F32),
            pltpu.VMEM((out_frames, 4, 128, c3), BF16),
            pltpu.VMEM((3, 3, 3, c2, c3), BF16),
            pltpu.SemaphoreType.DMA,
            pltpu.SemaphoreType.DMA((4,)),
        ],
        compiler_params=pltpu.CompilerParams(vmem_limit_bytes=16 * 1024 * 1024),
        cost_estimate=pl.CostEstimate(
            flops=4_000_000_000, bytes_accessed=10_000_000, transcendentals=600_000
        ),
    )(held, received, *first, *taps, *in_hbm(k3))


def solution(mesh):
    placed = (P(None, AXES), P(), P(), P(), P(), P(), P(), P(), P())
    return jax.shard_map(
        per_device,
        mesh=mesh,
        in_specs=placed,
        out_specs=P("tm", "seq", None, None),
        check_vma=False,
    )
```

```python
import functools

import jax
import jax.numpy as jnp
from jax import lax
from jax.experimental import pallas as pl
from jax.experimental.pallas import tpu as pltpu
from jax.sharding import PartitionSpec as P

F32, BF16 = jnp.float32, jnp.bfloat16
AXES = ("seq", "tm")


def hop(array, partner, seq, tm):
    pairs = []
    for s in range(seq):
        for t in range(tm):
            s2, t2 = partner(s, t)
            pairs.append((s * tm + t, s2 * tm + t2))
    return lax.ppermute(array, AXES, pairs)


def gathered_pieces(latent, k1, b1, g1, b2, g2, b3):
    seq, tm = lax.axis_size("seq"), lax.axis_size("tm")
    assert seq % 2 == 0 and tm == 4

    def z_partner(first):
        def partner(s, t):
            z = s // 2
            other = z + 1 if (z - first) % 2 == 0 else z - 1
            return (s + 2 * (other - z), t ^ 1) if 0 <= other < seq // 2 else (s, t ^ 1)

        return partner

    beside = hop(latent[None], lambda s, t: (s, t ^ 3), seq, tm)
    *first, own = fetched_first(k1, b1, g1, b2, g2, b3, latent)
    beside, own, *first = lax.optimization_barrier((beside, own, *first))
    held = jnp.concatenate([own, beside])
    held = jnp.concatenate([held, hop(held, lambda s, t: (s ^ 1, t ^ 1), seq, tm)])
    even = hop(held, z_partner(0), seq, tm)
    odd = hop(held, z_partner(1), seq, tm)
    held = jnp.concatenate([held, even, odd])
    return held, hop(held, lambda s, t: (s, t ^ 1), seq, tm), first


def normed(hidden, gain):
    factor = lax.rsqrt(jnp.mean(hidden * hidden, axis=-1, keepdims=True) + 1e-06)
    half = hidden * (0.5 * factor) * gain
    return (half + half * jnp.tanh(half)).astype(BF16)


def first_weights_kernel(
    k1, b1_in, g1_in, b2_in, g2_in, b3_in, latent, w1, b1, g1, b2, g2, b3, own, sem
):
    pairs = [(b1_in, b1), (g1_in, g1), (b2_in, b2), (g2_in, g2), (b3_in, b3)]
    pairs.append((latent, own.at[0]))
    for i in range(3):
        for j in range(3):
            pairs.append((k1.at[i, j], w1.at[pl.ds(i * 256 + j * 64, 48)]))
    copies = [pltpu.make_async_copy(a, b, sem.at[n]) for n, (a, b) in enumerate(pairs)]
    for copy in copies:
        copy.start()
    for i in range(3):
        for start, size in ((48, 16), (112, 16), (176, 80)):
            w1[pl.ds(i * 256 + start, size), :] = jnp.zeros((size, w1.shape[1]), BF16)
    for copy in copies:
        copy.wait()


def in_hbm(*arrays):
    return [pltpu.with_memory_space_constraint(array, pltpu.HBM) for array in arrays]


def fetched_first(k1, b1, g1, b2, g2, b3, latent):
    c1 = k1.shape[4]
    rows = [v.reshape(1, -1) for v in (b1, g1, b2, g2, b3)]
    shapes = [pltpu.VMEM((768, c1), BF16)] + [pltpu.VMEM(v.shape, F32) for v in rows]
    return pl.pallas_call(
        first_weights_kernel,
        out_shape=shapes + [pltpu.VMEM((1,) + latent.shape, BF16)],
        in_specs=[pl.BlockSpec(memory_space=pltpu.HBM)] * 7,
        out_specs=[pl.BlockSpec(memory_space=pltpu.VMEM)] * 7,
        scratch_shapes=[pltpu.SemaphoreType.DMA((15,))],
        compiler_params=pltpu.CompilerParams(vmem_limit_bytes=1024 * 1024),
        cost_estimate=pl.CostEstimate(flops=10000000000, bytes_accessed=40000000, transcendentals=0),
    )(*in_hbm(k1.reshape(3, 3, 48, c1), *rows, latent))


def decode_kernel(
    rows_total,
    held,
    received,
    w1,
    b1,
    g1,
    b2,
    g2,
    b3,
    w2,
    w3,
    out_hbm,
    pieces,
    rolled,
    rolled_far,
    patches,
    first_act,
    edge,
    middle_sums,
    second_act,
    final,
    line,
    out,
    sem_out,
):
    s = lax.axis_index("seq")
    t = lax.axis_index("tm")
    z, x, y, c = s // 2, s % 2, t // 2, t % 2
    n_frames = held.shape[1]
    pieces[:12] = held[...].astype(F32)
    pieces[12:] = received[...].astype(F32)

    def piece_of(row, chunk):
        dz, dx = row // 2 - z, row % 2 ^ x
        dy, dc = chunk // 2 ^ y, chunk % 2 ^ c
        group = jnp.where(dz == 0, 0, jnp.where((dz == 1) == (z % 2 == 0), 1, 2))
        half = (dx + dy + dc + jnp.where(dz == 0, 0, 1)) % 2
        return half * 12 + group * 4 + 2 * dx + dy

    lane = lax.broadcasted_iota(jnp.int32, (n_frames, 128), 1)

    def one_row(d, _):
        row = jnp.clip(s - 2 + d, 0, rows_total - 1)
        chunks = [pieces[piece_of(row, chunk)] for chunk in range(4)]
        for chunk in range(4):
            for q in range(8):
                shift = (16 - 16 * q) % 128
                near = pltpu.roll(chunks[chunk], shift, 1) if shift else chunks[chunk]
                if q == 0:
                    before = pltpu.roll(chunks[chunk - 1], 16, 1) if chunk else chunks[0]
                    near = jnp.where(lane < 16, before, near)
                if q == 7:
                    after = chunks[chunk + 1] if chunk < 3 else chunks[3]
                    after = pltpu.roll(after, 32 if chunk < 3 else 48, 1)
                    near = jnp.where((lane >= 32) & (lane < 48), after, near)
                at = pl.ds(d * n_frames * 32 + 8 * chunk + q, n_frames, stride=32)
                rolled[at, :] = near
                rolled_far[at, :] = pltpu.roll(near, 64, 1)
        return 0

    lax.fori_loop(0, 5, one_row, 0)

    left = lax.broadcasted_iota(jnp.int32, (32, 128), 1) < 64

    def one_patch(r, _):
        mine = jnp.clip(s - 1 + r, 0, rows_total - 1)
        d = [jnp.clip(mine - 1 + j, 0, rows_total - 1) - (s - 2) for j in range(3)]
        for w in range(8):
            frame = jnp.maximum(2 * t - 6 + w, 0)
            at = [pl.ds(pl.multiple_of((d[j] * n_frames + frame) * 32, 32), 32) for j in range(3)]
            pair = jnp.where(left, rolled[at[0], :], rolled_far[at[1], :])
            patches[r, w, :, :128] = pair.astype(BF16)
            patches[r, w, :, 128:] = rolled[at[2], :].astype(BF16)
        return 0

    lax.fori_loop(0, 3, one_patch, 0)

    def first(r):
        lhs = jnp.concatenate([patches[r, i : i + 6].reshape(192, 256) for i in range(3)], axis=1)
        hidden = jnp.dot(lhs, w1[...], preferred_element_type=F32) + b1[...]
        first_act[r] = normed(hidden, g1[...]).reshape(6, 32, 512)

    for r in range(3):
        first(r)

    def lhs(rows):
        m = (rows.stop - rows.start) * 128
        return [first_act[rows, i : i + 4].reshape(m, 512) for i in range(3)]

    for k in range(3):
        edge[k] = jnp.dot(
            jnp.concatenate(lhs(slice(0, 2)) + lhs(slice(1, 3)), axis=1),
            jnp.concatenate([w2[i, j, k] for j in (0, 2) for i in range(3)], axis=0),
            preferred_element_type=F32,
        )
    for k in range(3):
        middle = jnp.dot(
            jnp.concatenate(lhs(slice(0, 3)), axis=1),
            jnp.concatenate([w2[i, 1, k] for i in range(3)], axis=0),
            preferred_element_type=F32,
        )
        middle_sums[k] = middle

    column = lax.broadcasted_iota(jnp.int32, (4, 32, 256), 1)

    def second_norm(p):
        e, m = p // 2 * 128, (p + 1) // 2 * 128
        a, b, d = [
            (edge[k, e : e + 128] + middle_sums[k, m : m + 128]).reshape(4, 32, 256)
            for k in range(3)
        ]
        a_left = jnp.where(column == 0, a, pltpu.roll(a, 1, 1))
        d_right = jnp.where(column == 31, d, pltpu.roll(d, 31, 1))
        second_act[p, 0] = normed(a_left + (b + b2[...]) + d, g2[...])
        second_act[p, 1] = normed(a + (b + b2[...]) + d_right, g2[...])

    for p in range(4):
        second_norm(p)


    def lhs3(rows):
        m = (rows.stop - rows.start) * 128
        return [second_act[rows, :, i : i + 2].reshape(m, 256) for i in range(3)]

    def taps(j):
        return jnp.concatenate(
            [jnp.concatenate([w3[i, j, k] for k in range(3)], axis=1) for i in range(3)], axis=0
        )

    outer3 = jnp.dot(
        jnp.concatenate(lhs3(slice(0, 3)) + lhs3(slice(1, 4)), axis=1),
        jnp.concatenate([taps(0), taps(2)], axis=0),
        preferred_element_type=F32,
    )
    middle = jnp.dot(
        jnp.concatenate(lhs3(slice(1, 3)), axis=1), taps(1), preferred_element_type=F32
    )
    for r in range(4):
        e, m = (r + 1) // 2, r // 2
        final[r] = outer3[e * 128 : (e + 1) * 128] + middle[m * 128 : (m + 1) * 128]

    narrow = lax.broadcasted_iota(jnp.int32, (32, 128), 0)

    def last(r):
        def part(q, g, k):
            return final[r, pl.ds((q * 2 + g) * 32, 32), k * 128 : (k + 1) * 128]

        for g in range(2):
            a0, a1, b0, b1_, d0, d1 = [part(q, g, k) for k in range(3) for q in range(2)]
            a_left = jnp.where(narrow == 0, a0, pltpu.roll(a1, 1, 0))
            d_right = jnp.where(narrow == 31, d1, pltpu.roll(d0, 31, 0))
            columns = (a_left + b0 + d0, a0 + b0 + d1, a0 + b1_ + d1, a1 + b1_ + d_right)
            for u, value in enumerate(columns):
                line[g, pl.ds(u, 32, stride=4), :] = value + b3[...]
            out[g, r] = line[g].astype(BF16)
        pltpu.make_async_copy(out.at[:, r], out_hbm.at[:, r], sem_out.at[r]).start()

    for r in range(4):
        last(r)
    for r in range(4):
        pltpu.make_async_copy(out.at[:, r], out_hbm.at[:, r], sem_out.at[r]).wait()


def per_device(latent, k1, b1, g1, k2, b2, g2, k3, b3):
    frames, lanes = latent.shape
    tm = lax.axis_size("tm")
    rows_total = lax.axis_size("seq")
    c1, c2, c3 = k1.shape[4], k2.shape[4], k3.shape[4]
    held, received, first = gathered_pieces(latent, k1, b1, g1, b2, g2, b3)
    vmem = pl.BlockSpec(memory_space=pltpu.VMEM)
    hbm = pl.BlockSpec(memory_space=pltpu.HBM)
    out_frames = frames // tm
    return pl.pallas_call(
        functools.partial(decode_kernel, rows_total),
        out_shape=jax.ShapeDtypeStruct((out_frames, 4, 128, c3), BF16),
        in_specs=[vmem] * 10,
        out_specs=hbm,
        scratch_shapes=[
            pltpu.VMEM((24, frames, 128), F32),
            pltpu.VMEM((5 * frames * 32, 128), F32),
            pltpu.VMEM((5 * frames * 32, 128), F32),
            pltpu.VMEM((3, 8, 32, 256), BF16),
            pltpu.VMEM((3, 6, 32, c1), BF16),
            pltpu.VMEM((3, 256, c2), F32),
            pltpu.VMEM((3, 384, c2), F32),
            pltpu.VMEM((4, 2, 4, 32, c2), BF16),
            pltpu.VMEM((4, 128, 3 * c3), F32),
            pltpu.VMEM((2, 128, c3), F32),
            pltpu.VMEM((out_frames, 4, 128, c3), BF16),
            pltpu.SemaphoreType.DMA((4,)),
        ],
        compiler_params=pltpu.CompilerParams(vmem_limit_bytes=12 * 1024 * 1024),
        cost_estimate=pl.CostEstimate(
            flops=4_000_000_000, bytes_accessed=10_000_000, transcendentals=600_000
        ),
    )(held, received, *first, k2, k3)


def solution(mesh):
    placed = (P(None, AXES), P(), P(), P(), P(), P(), P(), P(), P())
    return jax.shard_map(
        per_device,
        mesh=mesh,
        in_specs=placed,
        out_specs=P("tm", "seq", None, None),
        check_vma=False,
    )
```

```python
import functools

import jax
import jax.numpy as jnp
from jax import lax
from jax.experimental import pallas as pl
from jax.experimental.pallas import tpu as pltpu
from jax.sharding import PartitionSpec as P

F32, BF16 = jnp.float32, jnp.bfloat16
AXES = ("seq", "tm")


def hop(array, partner, seq, tm):
    pairs = []
    for s in range(seq):
        for t in range(tm):
            s2, t2 = partner(s, t)
            pairs.append((s * tm + t, s2 * tm + t2))
    return lax.ppermute(array, AXES, pairs)


def gathered_pieces(latent, k1, b1, g1, b2, g2, b3):
    seq, tm = lax.axis_size("seq"), lax.axis_size("tm")
    assert seq % 2 == 0 and tm == 4

    def z_partner(first):
        def partner(s, t):
            z = s // 2
            other = z + 1 if (z - first) % 2 == 0 else z - 1
            return (s + 2 * (other - z), t ^ 1) if 0 <= other < seq // 2 else (s, t ^ 1)

        return partner

    beside = hop(latent[None], lambda s, t: (s, t ^ 3), seq, tm)
    *first, own = fetched_first(k1, b1, g1, b2, g2, b3, latent)
    beside, own, *first = lax.optimization_barrier((beside, own, *first))
    held = jnp.concatenate([own, beside])
    held = jnp.concatenate([held, hop(held, lambda s, t: (s ^ 1, t ^ 1), seq, tm)])
    even = hop(held, z_partner(0), seq, tm)
    odd = hop(held, z_partner(1), seq, tm)
    held = jnp.concatenate([held, even, odd])
    return held, hop(held, lambda s, t: (s, t ^ 1), seq, tm), first


def normed(hidden, gain):
    factor = lax.rsqrt(jnp.mean(hidden * hidden, axis=-1, keepdims=True) + 1e-06)
    half = hidden * (0.5 * factor) * gain
    return (half + half * jnp.tanh(half)).astype(BF16)


def first_weights_kernel(
    k1, b1_in, g1_in, b2_in, g2_in, b3_in, latent, w1, b1, g1, b2, g2, b3, own, sem
):
    pairs = [(b1_in, b1), (g1_in, g1), (b2_in, b2), (g2_in, g2), (b3_in, b3)]
    pairs.append((latent, own.at[0]))
    for i in range(3):
        pairs.append((k1.at[i], w1.at[pl.ds(0, 9), pl.ds(16 * (1 + i), 16)]))
    copies = [pltpu.make_async_copy(a, b, sem.at[n]) for n, (a, b) in enumerate(pairs)]
    for copy in copies:
        copy.start()
    zeros = jnp.zeros((9, 16, w1.shape[2]), BF16)
    w1[:9, :16] = zeros
    w1[:9, 64:] = zeros
    w1[9] = jnp.zeros(w1.shape[1:], BF16)
    for copy in copies:
        copy.wait()


def in_hbm(*arrays):
    return [pltpu.with_memory_space_constraint(array, pltpu.HBM) for array in arrays]


def fetched_first(k1, b1, g1, b2, g2, b3, latent):
    c1 = k1.shape[4]
    rows = [v.reshape(1, -1) for v in (b1, g1, b2, g2, b3)]
    shapes = [pltpu.VMEM((10, 80, c1), BF16)] + [pltpu.VMEM(v.shape, F32) for v in rows]
    return pl.pallas_call(
        first_weights_kernel,
        out_shape=shapes + [pltpu.VMEM((1,) + latent.shape, BF16)],
        in_specs=[pl.BlockSpec(memory_space=pltpu.HBM)] * 7,
        out_specs=[pl.BlockSpec(memory_space=pltpu.VMEM)] * 7,
        scratch_shapes=[pltpu.SemaphoreType.DMA((9,))],
        compiler_params=pltpu.CompilerParams(vmem_limit_bytes=1024 * 1024),
        cost_estimate=pl.CostEstimate(flops=10000000000, bytes_accessed=40000000, transcendentals=0),
    )(*in_hbm(k1.reshape(3, 9, 16, c1), *rows, latent))


def decode_kernel(
    rows_total,
    held,
    received,
    w1,
    b1,
    g1,
    b2,
    g2,
    b3,
    w2,
    w3,
    out_hbm,
    pieces,
    shifted,
    patches,
    first_act,
    edge,
    middle_sums,
    second_act,
    outer3,
    middle3,
    line,
    out,
    sem_out,
):
    s = lax.axis_index("seq")
    t = lax.axis_index("tm")
    z, x, y, c = s // 2, s % 2, t // 2, t % 2
    n_frames = held.shape[1]
    pieces[:12] = held[...].astype(F32)
    pieces[12:] = received[...].astype(F32)

    def piece_of(row, chunk):
        dz, dx = row // 2 - z, row % 2 ^ x
        dy, dc = chunk // 2 ^ y, chunk % 2 ^ c
        group = jnp.where(dz == 0, 0, jnp.where((dz == 1) == (z % 2 == 0), 1, 2))
        half = (dx + dy + dc + jnp.where(dz == 0, 0, 1)) % 2
        return half * 12 + group * 4 + 2 * dx + dy

    before = n_frames - 2 - 2 * t
    frame = lax.broadcasted_iota(jnp.int32, (4, n_frames, 128), 1)
    group = lax.broadcasted_iota(jnp.int32, (4, n_frames, 128), 2) // 16
    column32 = lax.broadcasted_iota(jnp.int32, (32, 128), 0)
    for d in range(5):
        row = jnp.clip(s - 2 + d, 0, rows_total - 1)
        block = jnp.stack([pieces[piece_of(row, chunk)] for chunk in range(4)])
        block = jnp.where(frame < before, block[:, :1], pltpu.roll(block, before, 1))
        for bit in (4, 2, 1):
            upper = pltpu.roll(pltpu.roll(block, 8 - bit, 1), 16 * bit, 2)
            lower = upper if bit == 4 else pltpu.roll(pltpu.roll(block, bit, 1), 128 - 16 * bit, 2)
            f, g = (frame & bit) != 0, (group & bit) != 0
            block = jnp.where(f == g, block, jnp.where(f, lower, upper))
        middle = block.reshape(32, 128)
        left = jnp.where(column32 == 0, middle, pltpu.roll(middle, 1, 0))
        right = jnp.where(column32 == 31, middle, pltpu.roll(middle, 31, 0))
        for k, value in enumerate((left, middle, right)):
            for n, turn in enumerate((0, 96, 64, 32)):
                turned = pltpu.roll(value, turn, 1) if turn else value
                shifted[n, d, k] = turned.astype(BF16)

    low = lax.broadcasted_iota(jnp.int32, (32, 128), 1) < 64
    for r in range(3):
        mine = jnp.clip(s - 1 + r, 0, rows_total - 1)
        d = [jnp.clip(mine - 1 + j, 0, rows_total - 1) - (s - 2) for j in range(3)]
        for n in range(5):
            first, second = 2 * n, min(2 * n + 1, 8)
            for v in range(3):
                one = shifted[v, d[first // 3], first % 3]
                two = shifted[(v + 2) % 4, d[second // 3], second % 3]
                patches[v, r, :, n * 128 : (n + 1) * 128] = jnp.where(low, one, two)

    for b in range(2):
        window = slice(16 - 16 * b, 80 - 16 * b)
        hidden = jnp.dot(
            patches[...].reshape(288, 640),
            jnp.concatenate([w1[n, window] for n in range(10)], axis=0),
            preferred_element_type=F32,
        )
        act = normed(hidden + b1[...], g1[...]).reshape(3, 3, 32, 512)
        for v in range(3):
            first_act[:, 2 * v + b] = act[v]

    def lhs(rows):
        m = (rows.stop - rows.start) * 128
        return [first_act[rows, i : i + 4].reshape(m, 512) for i in range(3)]

    def taps2(i, j):
        return jnp.concatenate([w2[i, j, k] for k in range(3)], axis=1)

    edge[...] = jnp.dot(
        jnp.concatenate(lhs(slice(0, 2)) + lhs(slice(1, 3)), axis=1),
        jnp.concatenate([taps2(i, j) for j in (0, 2) for i in range(3)], axis=0),
        preferred_element_type=F32,
    )
    middle_sums[...] = jnp.dot(
        jnp.concatenate(lhs(slice(0, 3)), axis=1),
        jnp.concatenate([taps2(i, 1) for i in range(3)], axis=0),
        preferred_element_type=F32,
    )

    column = lax.broadcasted_iota(jnp.int32, (4, 32, 256), 1)

    def second_norm(p):
        e, m = p // 2 * 128, (p + 1) // 2 * 128
        a, b, d = [
            (edge[e : e + 128, lanes] + middle_sums[m : m + 128, lanes]).reshape(4, 32, 256)
            for lanes in (slice(k * 256, (k + 1) * 256) for k in range(3))
        ]
        a_left = jnp.where(column == 0, a, pltpu.roll(a, 1, 1))
        d_right = jnp.where(column == 31, d, pltpu.roll(d, 31, 1))
        second_act[p, 0] = normed(a_left + (b + b2[...]) + d, g2[...])
        second_act[p, 1] = normed(a + (b + b2[...]) + d_right, g2[...])

    for p in range(4):
        second_norm(p)


    def lhs3(rows):
        m = (rows.stop - rows.start) * 128
        return [second_act[rows, :, i : i + 2].reshape(m, 256) for i in range(3)]

    def block3(j, ks):
        return jnp.concatenate(
            [jnp.concatenate([w3[i, j, k] for k in ks], axis=1) for i in range(3)], axis=0
        )

    none = jnp.zeros((768, 128), BF16)
    upper = jnp.concatenate([block3(0, (0, 1, 2)), block3(1, (2,))], axis=1)
    lower = jnp.concatenate([block3(2, (0, 1, 2)), none], axis=1)
    outer3[...] = jnp.dot(
        jnp.concatenate(lhs3(slice(0, 3)) + lhs3(slice(1, 4)), axis=1),
        jnp.concatenate([upper, lower], axis=0),
        preferred_element_type=F32,
    )
    middle3[...] = jnp.dot(
        jnp.concatenate(lhs3(slice(1, 3)), axis=1), block3(1, (0, 1)), preferred_element_type=F32
    )
    narrow = lax.broadcasted_iota(jnp.int32, (32, 128), 0)

    def last(r):
        def part(q, g, k):
            e, m, at = (r + 1) // 2 * 128, r // 2 * 128, (q * 2 + g) * 32
            outer = outer3[e + at : e + at + 32, k * 128 : (k + 1) * 128]
            if k == 2:
                return outer + outer3[m + 128 + at : m + 160 + at, 384:]
            return outer + middle3[m + at : m + at + 32, k * 128 : (k + 1) * 128]

        for g in range(2):
            a0, a1, b0, b1_, d0, d1 = [part(q, g, k) for k in range(3) for q in range(2)]
            a_left = jnp.where(narrow == 0, a0, pltpu.roll(a1, 1, 0))
            d_right = jnp.where(narrow == 31, d1, pltpu.roll(d0, 31, 0))
            columns = (a_left + b0 + d0, a0 + b0 + d1, a0 + b1_ + d1, a1 + b1_ + d_right)
            for u, value in enumerate(columns):
                line[g, pl.ds(u, 32, stride=4), :] = value + b3[...]
            out[g, r] = line[g].astype(BF16)
        pltpu.make_async_copy(out.at[:, r], out_hbm.at[:, r], sem_out.at[r]).start()

    for r in range(4):
        last(r)
    for r in range(4):
        pltpu.make_async_copy(out.at[:, r], out_hbm.at[:, r], sem_out.at[r]).wait()


def per_device(latent, k1, b1, g1, k2, b2, g2, k3, b3):
    frames, lanes = latent.shape
    tm = lax.axis_size("tm")
    rows_total = lax.axis_size("seq")
    c1, c2, c3 = k1.shape[4], k2.shape[4], k3.shape[4]
    held, received, first = gathered_pieces(latent, k1, b1, g1, b2, g2, b3)
    vmem = pl.BlockSpec(memory_space=pltpu.VMEM)
    hbm = pl.BlockSpec(memory_space=pltpu.HBM)
    out_frames = frames // tm
    return pl.pallas_call(
        functools.partial(decode_kernel, rows_total),
        out_shape=jax.ShapeDtypeStruct((out_frames, 4, 128, c3), BF16),
        in_specs=[vmem] * 10,
        out_specs=hbm,
        scratch_shapes=[
            pltpu.VMEM((24, frames, 128), F32),
            pltpu.VMEM((4, 5, 3, 32, 128), BF16),
            pltpu.VMEM((3, 3, 32, 640), BF16),
            pltpu.VMEM((3, 6, 32, c1), BF16),
            pltpu.VMEM((256, 3 * c2), F32),
            pltpu.VMEM((384, 3 * c2), F32),
            pltpu.VMEM((4, 2, 4, 32, c2), BF16),
            pltpu.VMEM((384, 4 * c3), F32),
            pltpu.VMEM((256, 2 * c3), F32),
            pltpu.VMEM((2, 128, c3), F32),
            pltpu.VMEM((out_frames, 4, 128, c3), BF16),
            pltpu.SemaphoreType.DMA((4,)),
        ],
        compiler_params=pltpu.CompilerParams(vmem_limit_bytes=12 * 1024 * 1024),
        cost_estimate=pl.CostEstimate(
            flops=4_000_000_000, bytes_accessed=10_000_000, transcendentals=600_000
        ),
    )(held, received, *first, k2, k3)


def solution(mesh):
    placed = (P(None, AXES), P(), P(), P(), P(), P(), P(), P(), P())
    return jax.shard_map(
        per_device,
        mesh=mesh,
        in_specs=placed,
        out_specs=P("tm", "seq", None, None),
        check_vma=False,
    )
```

```python
import functools

import jax
import jax.numpy as jnp
from jax import lax
from jax.experimental import pallas as pl
from jax.experimental.pallas import tpu as pltpu
from jax.sharding import PartitionSpec as P

F32, BF16 = jnp.float32, jnp.bfloat16
AXES = ("seq", "tm")


def hop(array, partner, seq, tm):
    pairs = []
    for s in range(seq):
        for t in range(tm):
            s2, t2 = partner(s, t)
            pairs.append((s * tm + t, s2 * tm + t2))
    return lax.ppermute(array, AXES, pairs)


def gathered_pieces(latent, k1, b1, g1, k2, b2, g2, b3):
    seq, tm = lax.axis_size("seq"), lax.axis_size("tm")
    assert seq % 2 == 0 and tm == 4

    def z_partner(first):
        def partner(s, t):
            z = s // 2
            other = z + 1 if (z - first) % 2 == 0 else z - 1
            return (s + 2 * (other - z), t ^ 1) if 0 <= other < seq // 2 else (s, t ^ 1)

        return partner

    beside = hop(latent[None], lambda s, t: (s, t ^ 3), seq, tm)
    *first, own = fetched_first(k1, b1, g1, b2, g2, b3, latent)
    beside, own, *first = lax.optimization_barrier((beside, own, *first))
    held = jnp.concatenate([own, beside])
    k2, _ = lax.optimization_barrier((k2, beside))
    across = hop(held, lambda s, t: (s ^ 1, t ^ 1), seq, tm)
    across, *sums0 = lax.optimization_barrier((across, *tap_sums(k2, 0)))
    held = jnp.concatenate([held, across])
    k2, _ = lax.optimization_barrier((k2, across))
    even = hop(held, z_partner(0), seq, tm)
    odd = hop(held, z_partner(1), seq, tm)
    even, odd, *sums1 = lax.optimization_barrier((even, odd, *tap_sums(k2, 1)))
    held = jnp.concatenate([held, even, odd])
    k2, _ = lax.optimization_barrier((k2, even))
    received = hop(held, lambda s, t: (s, t ^ 1), seq, tm)
    sums2 = tap_sums(k2, 2)
    return held, received, first, [*sums0, *sums1, *sums2], k2


def normed(hidden, gain):
    factor = lax.rsqrt(jnp.mean(hidden * hidden, axis=-1, keepdims=True) + 1e-06)
    half = hidden * (0.5 * factor) * gain
    return (half + half * jnp.tanh(half)).astype(BF16)


def first_weights_kernel(
    k1, b1_in, g1_in, b2_in, g2_in, b3_in, latent, w1, b1, g1, b2, g2, b3, own, sem
):
    pairs = [(b1_in, b1), (g1_in, g1), (b2_in, b2), (g2_in, g2), (b3_in, b3)]
    pairs.append((latent, own.at[0]))
    for i in range(3):
        pairs.append((k1.at[i], w1.at[pl.ds(0, 9), pl.ds(16 * (1 + i), 16)]))
    copies = [pltpu.make_async_copy(a, b, sem.at[n]) for n, (a, b) in enumerate(pairs)]
    for copy in copies:
        copy.start()
    zeros = jnp.zeros((9, 16, w1.shape[2]), BF16)
    w1[:9, :16] = zeros
    w1[:9, 64:] = zeros
    w1[9] = jnp.zeros(w1.shape[1:], BF16)
    for copy in copies:
        copy.wait()


def in_hbm(*arrays):
    return [pltpu.with_memory_space_constraint(array, pltpu.HBM) for array in arrays]


def fetched_first(k1, b1, g1, b2, g2, b3, latent):
    c1 = k1.shape[4]
    rows = [v.reshape(1, -1) for v in (b1, g1, b2, g2, b3)]
    shapes = [pltpu.VMEM((10, 80, c1), BF16)] + [pltpu.VMEM(v.shape, F32) for v in rows]
    return pl.pallas_call(
        first_weights_kernel,
        out_shape=shapes + [pltpu.VMEM((1,) + latent.shape, BF16)],
        in_specs=[pl.BlockSpec(memory_space=pltpu.HBM)] * 7,
        out_specs=[pl.BlockSpec(memory_space=pltpu.VMEM)] * 7,
        scratch_shapes=[pltpu.SemaphoreType.DMA((9,))],
        compiler_params=pltpu.CompilerParams(vmem_limit_bytes=1024 * 1024),
        cost_estimate=pl.CostEstimate(flops=10000000000, bytes_accessed=40000000, transcendentals=0),
    )(*in_hbm(k1.reshape(3, 9, 16, c1), *rows, latent))


def tap_sums_kernel(i, k2, low, high, full):
    def part(n, _):
        k, at = n // 8, pl.ds(pl.multiple_of(n % 8 * 64, 64), 64)
        a, b, c = [k2[i, j, k, at, :].astype(F32) for j in range(3)]
        ab = a + b
        low[k, at, :] = ab.astype(BF16)
        high[k, at, :] = (b + c).astype(BF16)
        full[k, at, :] = (ab + c).astype(BF16)
        return 0

    lax.fori_loop(0, 24, part, 0)


def tap_sums(k2, i):
    vmem = pl.BlockSpec(memory_space=pltpu.VMEM)
    return pl.pallas_call(
        functools.partial(tap_sums_kernel, i),
        out_shape=[pltpu.VMEM(k2.shape[2:], BF16)] * 3,
        in_specs=[vmem],
        out_specs=[vmem] * 3,
        compiler_params=pltpu.CompilerParams(vmem_limit_bytes=1024 * 1024),
        cost_estimate=pl.CostEstimate(flops=0, bytes_accessed=4_000_000, transcendentals=0),
    )(k2)


def decode_kernel(
    rows_total,
    held,
    received,
    w1,
    b1,
    g1,
    b2,
    g2,
    b3,
    low0,
    high0,
    full0,
    low1,
    high1,
    full1,
    low2,
    high2,
    full2,
    w2,
    w3,
    out_hbm,
    pieces,
    shifted,
    patches,
    first_act,
    difference,
    upper_sums,
    middle_sums,
    lower_sums,
    second_act,
    outer3,
    middle3,
    line,
    out,
    sem_out,
):
    s = lax.axis_index("seq")
    t = lax.axis_index("tm")
    z, x, y, c = s // 2, s % 2, t // 2, t % 2
    n_frames = held.shape[1]
    pieces[:12] = held[...].astype(F32)
    pieces[12:] = received[...].astype(F32)

    def piece_of(row, chunk):
        dz, dx = row // 2 - z, row % 2 ^ x
        dy, dc = chunk // 2 ^ y, chunk % 2 ^ c
        group = jnp.where(dz == 0, 0, jnp.where((dz == 1) == (z % 2 == 0), 1, 2))
        half = (dx + dy + dc + jnp.where(dz == 0, 0, 1)) % 2
        return half * 12 + group * 4 + 2 * dx + dy

    before = n_frames - 2 - 2 * t
    frame = lax.broadcasted_iota(jnp.int32, (4, n_frames, 128), 1)
    group = lax.broadcasted_iota(jnp.int32, (4, n_frames, 128), 2) // 16
    column32 = lax.broadcasted_iota(jnp.int32, (32, 128), 0)
    for d in range(5):
        row = jnp.clip(s - 2 + d, 0, rows_total - 1)
        block = jnp.stack([pieces[piece_of(row, chunk)] for chunk in range(4)])
        block = jnp.where(frame < before, block[:, :1], pltpu.roll(block, before, 1))
        for bit in (4, 2, 1):
            upper = pltpu.roll(pltpu.roll(block, 8 - bit, 1), 16 * bit, 2)
            lower = upper if bit == 4 else pltpu.roll(pltpu.roll(block, bit, 1), 128 - 16 * bit, 2)
            f, g = (frame & bit) != 0, (group & bit) != 0
            block = jnp.where(f == g, block, jnp.where(f, lower, upper))
        middle = block.reshape(32, 128)
        left = jnp.where(column32 == 0, middle, pltpu.roll(middle, 1, 0))
        right = jnp.where(column32 == 31, middle, pltpu.roll(middle, 31, 0))
        for k, value in enumerate((left, middle, right)):
            for n, turn in enumerate((0, 96, 64, 32)):
                turned = pltpu.roll(value, turn, 1) if turn else value
                shifted[n, d, k] = turned.astype(BF16)

    low = lax.broadcasted_iota(jnp.int32, (32, 128), 1) < 64
    for r in range(3):
        mine = jnp.clip(s - 1 + r, 0, rows_total - 1)
        d = [jnp.clip(mine - 1 + j, 0, rows_total - 1) - (s - 2) for j in range(3)]
        for n in range(5):
            first, second = 2 * n, min(2 * n + 1, 8)
            for v in range(3):
                one = shifted[v, d[first // 3], first % 3]
                two = shifted[(v + 2) % 4, d[second // 3], second % 3]
                patches[v, r, :, n * 128 : (n + 1) * 128] = jnp.where(low, one, two)

    for b in range(2):
        window = slice(16 - 16 * b, 80 - 16 * b)
        hidden = jnp.dot(
            patches[...].reshape(288, 640),
            jnp.concatenate([w1[n, window] for n in range(10)], axis=0),
            preferred_element_type=F32,
        )
        act = normed(hidden + b1[...], g1[...]).reshape(3, 3, 32, 512)
        for v in range(3):
            first_act[:, 2 * v + b] = act[v]

    v0, v1, v2 = [first_act[r].astype(F32) for r in range(3)]
    difference[0] = (v0 - v1).astype(BF16)
    difference[1] = (v1 - v2).astype(BF16)

    def lhs(ref, r):
        return jnp.concatenate([ref[r, i : i + 4].reshape(128, 512) for i in range(3)], axis=1)

    def side_by_side(taps):
        return jnp.concatenate(
            [jnp.concatenate([tap[k] for tap in of_i for k in range(3)], axis=1) for of_i in taps],
            axis=0,
        )

    upper_sums[...] = jnp.dot(
        lhs(difference, 0),
        side_by_side([(low, w2.at[i, 0]) for i, low in enumerate((low0, low1, low2))]),
        preferred_element_type=F32,
    )
    middle_sums[...] = jnp.dot(
        lhs(first_act, 1),
        side_by_side([(full,) for full in (full0, full1, full2)]),
        preferred_element_type=F32,
    )
    lower_sums[...] = jnp.dot(
        lhs(difference, 1),
        side_by_side([(w2.at[i, 2], high) for i, high in enumerate((high0, high1, high2))]),
        preferred_element_type=F32,
    )

    column = lax.broadcasted_iota(jnp.int32, (4, 32, 256), 1)

    def second_norm(p):
        def sums(k):
            both, own = k * 256, (p % 2 * 3 + k) * 256
            shared = middle_sums[:, both : both + 256]
            if p < 2:
                total = shared + upper_sums[:, own : own + 256]
            else:
                total = shared - lower_sums[:, own : own + 256]
            return total.reshape(4, 32, 256)

        a, b, d = [sums(k) for k in range(3)]
        a_left = jnp.where(column == 0, a, pltpu.roll(a, 1, 1))
        d_right = jnp.where(column == 31, d, pltpu.roll(d, 31, 1))
        second_act[p, 0] = normed(a_left + (b + b2[...]) + d, g2[...])
        second_act[p, 1] = normed(a + (b + b2[...]) + d_right, g2[...])

    for p in range(4):
        second_norm(p)


    def lhs3(rows):
        m = (rows.stop - rows.start) * 128
        return [second_act[rows, :, i : i + 2].reshape(m, 256) for i in range(3)]

    def block3(j, ks):
        return jnp.concatenate(
            [jnp.concatenate([w3[i, j, k] for k in ks], axis=1) for i in range(3)], axis=0
        )

    none = jnp.zeros((768, 128), BF16)
    upper = jnp.concatenate([block3(0, (0, 1, 2)), block3(1, (2,))], axis=1)
    lower = jnp.concatenate([block3(2, (0, 1, 2)), none], axis=1)
    outer3[...] = jnp.dot(
        jnp.concatenate(lhs3(slice(0, 3)) + lhs3(slice(1, 4)), axis=1),
        jnp.concatenate([upper, lower], axis=0),
        preferred_element_type=F32,
    )
    middle3[...] = jnp.dot(
        jnp.concatenate(lhs3(slice(1, 3)), axis=1), block3(1, (0, 1)), preferred_element_type=F32
    )
    narrow = lax.broadcasted_iota(jnp.int32, (32, 128), 0)

    def last(r):
        def part(q, g, k):
            e, m, at = (r + 1) // 2 * 128, r // 2 * 128, (q * 2 + g) * 32
            outer = outer3[e + at : e + at + 32, k * 128 : (k + 1) * 128]
            if k == 2:
                return outer + outer3[m + 128 + at : m + 160 + at, 384:]
            return outer + middle3[m + at : m + at + 32, k * 128 : (k + 1) * 128]

        for g in range(2):
            a0, a1, b0, b1_, d0, d1 = [part(q, g, k) for k in range(3) for q in range(2)]
            a_left = jnp.where(narrow == 0, a0, pltpu.roll(a1, 1, 0))
            d_right = jnp.where(narrow == 31, d1, pltpu.roll(d0, 31, 0))
            columns = (a_left + b0 + d0, a0 + b0 + d1, a0 + b1_ + d1, a1 + b1_ + d_right)
            for u, value in enumerate(columns):
                line[g, pl.ds(u, 32, stride=4), :] = value + b3[...]
            out[g, r] = line[g].astype(BF16)
        pltpu.make_async_copy(out.at[:, r], out_hbm.at[:, r], sem_out.at[r]).start()

    for r in range(4):
        last(r)
    for r in range(4):
        pltpu.make_async_copy(out.at[:, r], out_hbm.at[:, r], sem_out.at[r]).wait()


def per_device(latent, k1, b1, g1, k2, b2, g2, k3, b3):
    frames, lanes = latent.shape
    tm = lax.axis_size("tm")
    rows_total = lax.axis_size("seq")
    c1, c2, c3 = k1.shape[4], k2.shape[4], k3.shape[4]
    held, received, first, sums, k2 = gathered_pieces(
        latent, k1, b1, g1, k2, b2, g2, b3
    )
    vmem = pl.BlockSpec(memory_space=pltpu.VMEM)
    hbm = pl.BlockSpec(memory_space=pltpu.HBM)
    out_frames = frames // tm
    return pl.pallas_call(
        functools.partial(decode_kernel, rows_total),
        out_shape=jax.ShapeDtypeStruct((out_frames, 4, 128, c3), BF16),
        in_specs=[vmem] * 19,
        out_specs=hbm,
        scratch_shapes=[
            pltpu.VMEM((24, frames, 128), F32),
            pltpu.VMEM((4, 5, 3, 32, 128), BF16),
            pltpu.VMEM((3, 3, 32, 640), BF16),
            pltpu.VMEM((3, 6, 32, c1), BF16),
            pltpu.VMEM((2, 6, 32, c1), BF16),
            pltpu.VMEM((128, 6 * c2), F32),
            pltpu.VMEM((128, 3 * c2), F32),
            pltpu.VMEM((128, 6 * c2), F32),
            pltpu.VMEM((4, 2, 4, 32, c2), BF16),
            pltpu.VMEM((384, 4 * c3), F32),
            pltpu.VMEM((256, 2 * c3), F32),
            pltpu.VMEM((2, 128, c3), F32),
            pltpu.VMEM((out_frames, 4, 128, c3), BF16),
            pltpu.SemaphoreType.DMA((4,)),
        ],
        compiler_params=pltpu.CompilerParams(vmem_limit_bytes=12 * 1024 * 1024),
        cost_estimate=pl.CostEstimate(
            flops=4_000_000_000, bytes_accessed=10_000_000, transcendentals=600_000
        ),
    )(held, received, *first, *sums, k2, k3)


def solution(mesh):
    placed = (P(None, AXES), P(), P(), P(), P(), P(), P(), P(), P())
    return jax.shard_map(
        per_device,
        mesh=mesh,
        in_specs=placed,
        out_specs=P("tm", "seq", None, None),
        check_vma=False,
    )
```

```python
import functools

import jax
import jax.numpy as jnp
from jax import lax
from jax.experimental import pallas as pl
from jax.experimental.pallas import tpu as pltpu
from jax.sharding import PartitionSpec as P

F32, BF16 = jnp.float32, jnp.bfloat16
AXES = ("seq", "tm")


def hop(array, partner, seq, tm):
    pairs = []
    for s in range(seq):
        for t in range(tm):
            s2, t2 = partner(s, t)
            pairs.append((s * tm + t, s2 * tm + t2))
    return lax.ppermute(array, AXES, pairs)


def gathered_pieces(latent, k1, b1, g1, k2, b2, g2, b3):
    seq, tm = lax.axis_size("seq"), lax.axis_size("tm")
    assert seq % 2 == 0 and tm == 4

    def z_partner(first):
        def partner(s, t):
            z = s // 2
            other = z + 1 if (z - first) % 2 == 0 else z - 1
            return (s + 2 * (other - z), t ^ 1) if 0 <= other < seq // 2 else (s, t ^ 1)

        return partner

    beside = hop(latent[None], lambda s, t: (s, t ^ 3), seq, tm)
    *first, own = fetched_first(k1, b1, g1, b2, g2, b3, latent)
    beside, own, *first = lax.optimization_barrier((beside, own, *first))
    held = jnp.concatenate([own, beside])
    k2, _ = lax.optimization_barrier((k2, beside))
    across = hop(held, lambda s, t: (s ^ 1, t ^ 1), seq, tm)
    across, *sums0 = lax.optimization_barrier((across, *tap_sums(k2, 0)))
    held = jnp.concatenate([held, across])
    k2, _ = lax.optimization_barrier((k2, across))
    even = hop(held, z_partner(0), seq, tm)
    odd = hop(held, z_partner(1), seq, tm)
    odd, even, *sums1 = lax.optimization_barrier((odd, even, *tap_sums(k2, 1)))
    held = jnp.concatenate([held, even, odd])
    k2, _ = lax.optimization_barrier((k2, even))
    received = hop(held, lambda s, t: (s, t ^ 1), seq, tm)
    sums2 = tap_sums(k2, 2)
    return held, received, first, [*sums0, *sums1, *sums2], k2


def normed(hidden, gain):
    factor = lax.rsqrt(jnp.mean(hidden * hidden, axis=-1, keepdims=True) + 1e-06)
    half = hidden * (0.5 * factor) * gain
    return (half + half * jnp.tanh(half)).astype(BF16)


def first_weights_kernel(
    k1, b1_in, g1_in, b2_in, g2_in, b3_in, latent, w1, b1, g1, b2, g2, b3, own, sem
):
    pairs = [(b1_in, b1), (g1_in, g1), (b2_in, b2), (g2_in, g2), (b3_in, b3)]
    pairs.append((latent, own.at[0]))
    for i in range(3):
        pairs.append((k1.at[i], w1.at[pl.ds(0, 9), pl.ds(16 * (1 + i), 16)]))
    copies = [pltpu.make_async_copy(a, b, sem.at[n]) for n, (a, b) in enumerate(pairs)]
    for copy in copies:
        copy.start()
    zeros = jnp.zeros((9, 16, w1.shape[2]), BF16)
    w1[:9, :16] = zeros
    w1[:9, 64:] = zeros
    w1[9] = jnp.zeros(w1.shape[1:], BF16)
    for copy in copies:
        copy.wait()


def in_hbm(*arrays):
    return [pltpu.with_memory_space_constraint(array, pltpu.HBM) for array in arrays]


def fetched_first(k1, b1, g1, b2, g2, b3, latent):
    c1 = k1.shape[4]
    rows = [v.reshape(1, -1) for v in (b1, g1, b2, g2, b3)]
    shapes = [pltpu.VMEM((10, 80, c1), BF16)] + [pltpu.VMEM(v.shape, F32) for v in rows]
    return pl.pallas_call(
        first_weights_kernel,
        out_shape=shapes + [pltpu.VMEM((1,) + latent.shape, BF16)],
        in_specs=[pl.BlockSpec(memory_space=pltpu.HBM)] * 7,
        out_specs=[pl.BlockSpec(memory_space=pltpu.VMEM)] * 7,
        scratch_shapes=[pltpu.SemaphoreType.DMA((9,))],
        compiler_params=pltpu.CompilerParams(vmem_limit_bytes=1024 * 1024),
        cost_estimate=pl.CostEstimate(flops=10000000000, bytes_accessed=40000000, transcendentals=0),
    )(*in_hbm(k1.reshape(3, 9, 16, c1), *rows, latent))


def tap_sums_kernel(i, k2, low, high, full):
    def part(n, _):
        k, at = n // 8, pl.ds(pl.multiple_of(n % 8 * 64, 64), 64)
        a, b, c = [k2[i, j, k, at, :].astype(F32) for j in range(3)]
        ab = a + b
        low[k, at, :] = ab.astype(BF16)
        high[k, at, :] = (b + c).astype(BF16)
        full[k, at, :] = (ab + c).astype(BF16)
        return 0

    lax.fori_loop(0, 24, part, 0)


def tap_sums(k2, i):
    vmem = pl.BlockSpec(memory_space=pltpu.VMEM)
    return pl.pallas_call(
        functools.partial(tap_sums_kernel, i),
        out_shape=[pltpu.VMEM(k2.shape[2:], BF16)] * 3,
        in_specs=[vmem],
        out_specs=[vmem] * 3,
        compiler_params=pltpu.CompilerParams(vmem_limit_bytes=1024 * 1024),
        cost_estimate=pl.CostEstimate(flops=0, bytes_accessed=4_000_000, transcendentals=0),
    )(k2)


def decode_kernel(
    rows_total,
    held,
    received,
    w1,
    b1,
    g1,
    b2,
    g2,
    b3,
    low0,
    high0,
    full0,
    low1,
    high1,
    full1,
    low2,
    high2,
    full2,
    w2,
    w3,
    out_hbm,
    pieces,
    shifted,
    patches,
    first_act,
    difference,
    upper_sums,
    middle_sums,
    lower_sums,
    second_act,
    outer3,
    middle3,
    line,
    out,
    sem_out,
):
    s = lax.axis_index("seq")
    t = lax.axis_index("tm")
    z, x, y, c = s // 2, s % 2, t // 2, t % 2
    n_frames = held.shape[1]
    pieces[:12] = held[...].astype(F32)
    pieces[12:] = received[...].astype(F32)

    def piece_of(row, chunk):
        dz, dx = row // 2 - z, row % 2 ^ x
        dy, dc = chunk // 2 ^ y, chunk % 2 ^ c
        group = jnp.where(dz == 0, 0, jnp.where((dz == 1) == (z % 2 == 0), 1, 2))
        half = (dx + dy + dc + jnp.where(dz == 0, 0, 1)) % 2
        return half * 12 + group * 4 + 2 * dx + dy

    before = n_frames - 2 - 2 * t
    frame = lax.broadcasted_iota(jnp.int32, (4, n_frames, 128), 1)
    group = lax.broadcasted_iota(jnp.int32, (4, n_frames, 128), 2) // 16
    column32 = lax.broadcasted_iota(jnp.int32, (32, 128), 0)
    for d in range(5):
        row = jnp.clip(s - 2 + d, 0, rows_total - 1)
        block = jnp.stack([pieces[piece_of(row, chunk)] for chunk in range(4)])
        block = jnp.where(frame < before, block[:, :1], pltpu.roll(block, before, 1))
        for bit in (4, 2, 1):
            upper = pltpu.roll(pltpu.roll(block, 8 - bit, 1), 16 * bit, 2)
            lower = upper if bit == 4 else pltpu.roll(pltpu.roll(block, bit, 1), 128 - 16 * bit, 2)
            f, g = (frame & bit) != 0, (group & bit) != 0
            block = jnp.where(f == g, block, jnp.where(f, lower, upper))
        middle = block.reshape(32, 128)
        left = jnp.where(column32 == 0, middle, pltpu.roll(middle, 1, 0))
        right = jnp.where(column32 == 31, middle, pltpu.roll(middle, 31, 0))
        for k, value in enumerate((left, middle, right)):
            for n, turn in enumerate((0, 96, 64, 32)):
                turned = pltpu.roll(value, turn, 1) if turn else value
                shifted[n, d, k] = turned.astype(BF16)

    low = lax.broadcasted_iota(jnp.int32, (32, 128), 1) < 64
    for r in range(3):
        mine = jnp.clip(s - 1 + r, 0, rows_total - 1)
        d = [jnp.clip(mine - 1 + j, 0, rows_total - 1) - (s - 2) for j in range(3)]
        for n in range(5):
            first, second = 2 * n, min(2 * n + 1, 8)
            for v in range(3):
                one = shifted[v, d[first // 3], first % 3]
                two = shifted[(v + 2) % 4, d[second // 3], second % 3]
                patches[v, r, :, n * 128 : (n + 1) * 128] = jnp.where(low, one, two)

    for b in range(2):
        window = slice(16 - 16 * b, 80 - 16 * b)
        hidden = jnp.dot(
            patches[...].reshape(288, 640),
            jnp.concatenate([w1[n, window] for n in range(10)], axis=0),
            preferred_element_type=F32,
        )
        act = normed(hidden + b1[...], g1[...]).reshape(3, 3, 32, 512)
        for v in range(3):
            first_act[:, 2 * v + b] = act[v]

    v0, v1, v2 = [first_act[r].astype(F32) for r in range(3)]
    difference[0] = (v0 - v1).astype(BF16)
    difference[1] = (v1 - v2).astype(BF16)

    def lhs(ref, r):
        return jnp.concatenate([ref[r, i : i + 4].reshape(128, 512) for i in range(3)], axis=1)

    def side_by_side(taps):
        return jnp.concatenate(
            [jnp.concatenate([tap[k] for tap in of_i for k in range(3)], axis=1) for of_i in taps],
            axis=0,
        )

    upper_sums[...] = jnp.dot(
        lhs(difference, 0),
        side_by_side([(low, w2.at[i, 0]) for i, low in enumerate((low0, low1, low2))]),
        preferred_element_type=F32,
    )
    middle_sums[...] = jnp.dot(
        lhs(first_act, 1),
        side_by_side([(full,) for full in (full0, full1, full2)]),
        preferred_element_type=F32,
    )
    lower_sums[...] = jnp.dot(
        lhs(difference, 1),
        side_by_side([(w2.at[i, 2], high) for i, high in enumerate((high0, high1, high2))]),
        preferred_element_type=F32,
    )

    column = lax.broadcasted_iota(jnp.int32, (4, 32, 256), 1)

    def second_norm(p):
        def sums(k):
            both, own = k * 256, (p % 2 * 3 + k) * 256
            shared = middle_sums[:, both : both + 256]
            if p < 2:
                total = shared + upper_sums[:, own : own + 256]
            else:
                total = shared - lower_sums[:, own : own + 256]
            return total.reshape(4, 32, 256)

        a, b, d = [sums(k) for k in range(3)]
        a_left = jnp.where(column == 0, a, pltpu.roll(a, 1, 1))
        d_right = jnp.where(column == 31, d, pltpu.roll(d, 31, 1))
        second_act[p, 0] = normed(a_left + (b + b2[...]) + d, g2[...])
        second_act[p, 1] = normed(a + (b + b2[...]) + d_right, g2[...])

    for p in range(4):
        second_norm(p)


    def lhs3(rows):
        m = (rows.stop - rows.start) * 128
        return [second_act[rows, :, i : i + 2].reshape(m, 256) for i in range(3)]

    def block3(j, ks):
        return jnp.concatenate(
            [jnp.concatenate([w3[i, j, k] for k in ks], axis=1) for i in range(3)], axis=0
        )

    none = jnp.zeros((768, 128), BF16)
    upper = jnp.concatenate([block3(0, (0, 1, 2)), block3(1, (2,))], axis=1)
    lower = jnp.concatenate([block3(2, (0, 1, 2)), none], axis=1)
    outer3[...] = jnp.dot(
        jnp.concatenate(lhs3(slice(0, 3)) + lhs3(slice(1, 4)), axis=1),
        jnp.concatenate([upper, lower], axis=0),
        preferred_element_type=F32,
    )
    middle3[...] = jnp.dot(
        jnp.concatenate(lhs3(slice(1, 3)), axis=1), block3(1, (0, 1)), preferred_element_type=F32
    )
    narrow = lax.broadcasted_iota(jnp.int32, (32, 128), 0)

    def last(r):
        def part(q, g, k):
            e, m, at = (r + 1) // 2 * 128, r // 2 * 128, (q * 2 + g) * 32
            outer = outer3[e + at : e + at + 32, k * 128 : (k + 1) * 128]
            if k == 2:
                return outer + outer3[m + 128 + at : m + 160 + at, 384:]
            return outer + middle3[m + at : m + at + 32, k * 128 : (k + 1) * 128]

        for g in range(2):
            a0, a1, b0, b1_, d0, d1 = [part(q, g, k) for k in range(3) for q in range(2)]
            a_left = jnp.where(narrow == 0, a0, pltpu.roll(a1, 1, 0))
            d_right = jnp.where(narrow == 31, d1, pltpu.roll(d0, 31, 0))
            columns = (a_left + b0 + d0, a0 + b0 + d1, a0 + b1_ + d1, a1 + b1_ + d_right)
            for u, value in enumerate(columns):
                line[g, pl.ds(u, 32, stride=4), :] = value + b3[...]
            out[g, r] = line[g].astype(BF16)
        pltpu.make_async_copy(out.at[:, r], out_hbm.at[:, r], sem_out.at[r]).start()

    for r in range(4):
        last(r)
    for r in range(4):
        pltpu.make_async_copy(out.at[:, r], out_hbm.at[:, r], sem_out.at[r]).wait()


def per_device(latent, k1, b1, g1, k2, b2, g2, k3, b3):
    frames, lanes = latent.shape
    tm = lax.axis_size("tm")
    rows_total = lax.axis_size("seq")
    c1, c2, c3 = k1.shape[4], k2.shape[4], k3.shape[4]
    held, received, first, sums, k2 = gathered_pieces(
        latent, k1, b1, g1, k2, b2, g2, b3
    )
    vmem = pl.BlockSpec(memory_space=pltpu.VMEM)
    hbm = pl.BlockSpec(memory_space=pltpu.HBM)
    out_frames = frames // tm
    return pl.pallas_call(
        functools.partial(decode_kernel, rows_total),
        out_shape=jax.ShapeDtypeStruct((out_frames, 4, 128, c3), BF16),
        in_specs=[vmem] * 19,
        out_specs=hbm,
        scratch_shapes=[
            pltpu.VMEM((24, frames, 128), F32),
            pltpu.VMEM((4, 5, 3, 32, 128), BF16),
            pltpu.VMEM((3, 3, 32, 640), BF16),
            pltpu.VMEM((3, 6, 32, c1), BF16),
            pltpu.VMEM((2, 6, 32, c1), BF16),
            pltpu.VMEM((128, 6 * c2), F32),
            pltpu.VMEM((128, 3 * c2), F32),
            pltpu.VMEM((128, 6 * c2), F32),
            pltpu.VMEM((4, 2, 4, 32, c2), BF16),
            pltpu.VMEM((384, 4 * c3), F32),
            pltpu.VMEM((256, 2 * c3), F32),
            pltpu.VMEM((2, 128, c3), F32),
            pltpu.VMEM((out_frames, 4, 128, c3), BF16),
            pltpu.SemaphoreType.DMA((4,)),
        ],
        compiler_params=pltpu.CompilerParams(vmem_limit_bytes=12 * 1024 * 1024),
        cost_estimate=pl.CostEstimate(
            flops=4_000_000_000, bytes_accessed=10_000_000, transcendentals=600_000
        ),
    )(held, received, *first, *sums, k2, k3)


def solution(mesh):
    placed = (P(None, AXES), P(), P(), P(), P(), P(), P(), P(), P())
    return jax.shard_map(
        per_device,
        mesh=mesh,
        in_specs=placed,
        out_specs=P("tm", "seq", None, None),
        check_vma=False,
    )
```

```python
import functools

import jax
import jax.numpy as jnp
from jax import lax
from jax.experimental import pallas as pl
from jax.experimental.pallas import tpu as pltpu
from jax.sharding import PartitionSpec as P

F32, BF16 = jnp.float32, jnp.bfloat16
AXES = ("seq", "tm")


def hop(array, partner, seq, tm):
    pairs = []
    for s in range(seq):
        for t in range(tm):
            s2, t2 = partner(s, t)
            pairs.append((s * tm + t, s2 * tm + t2))
    return lax.ppermute(array, AXES, pairs)


def gathered_pieces(latent, k1, b1, g1, k2, b2, g2, b3):
    seq, tm = lax.axis_size("seq"), lax.axis_size("tm")
    assert seq % 2 == 0 and tm == 4

    def z_partner(first):
        def partner(s, t):
            z = s // 2
            other = z + 1 if (z - first) % 2 == 0 else z - 1
            return (s + 2 * (other - z), t ^ 1) if 0 <= other < seq // 2 else (s, t ^ 1)

        return partner

    beside = hop(latent[None], lambda s, t: (s, t ^ 3), seq, tm)
    *first, own = fetched_first(k1, b1, g1, b2, g2, b3, latent)
    beside, own, *first = lax.optimization_barrier((beside, own, *first))
    held = jnp.concatenate([own, beside])
    k2, _ = lax.optimization_barrier((k2, beside))
    across = hop(held, lambda s, t: (s ^ 1, t ^ 1), seq, tm)
    across, *sums0 = lax.optimization_barrier((across, *tap_sums(k2, 0)))
    held = jnp.concatenate([held, across])
    k2, _ = lax.optimization_barrier((k2, across))
    even = hop(held, z_partner(0), seq, tm)
    odd = hop(held, z_partner(1), seq, tm)
    odd, even, *sums1 = lax.optimization_barrier((odd, even, *tap_sums(k2, 1)))
    held = jnp.concatenate([held, even, odd])
    k2, _ = lax.optimization_barrier((k2, even))
    received = hop(held, lambda s, t: (s, t ^ 1), seq, tm)
    sums2 = tap_sums(k2, 2)
    return held, received, first, [*sums0, *sums1, *sums2], k2


def normed(hidden, gain):
    factor = lax.rsqrt(jnp.mean(hidden * hidden, axis=-1, keepdims=True) + 1e-06)
    half = hidden * (0.5 * factor) * gain
    return (half + half * jnp.tanh(half)).astype(BF16)


def first_weights_kernel(
    k1, b1_in, g1_in, b2_in, g2_in, b3_in, latent, w1, b1, g1, b2, g2, b3, own, sem
):
    pairs = [(b1_in, b1), (g1_in, g1), (b2_in, b2), (g2_in, g2), (b3_in, b3)]
    pairs.append((latent, own.at[0]))
    for i in range(3):
        for n in range(9):
            pairs.append((k1.at[i, n], w1.at[pl.ds(48 * n + 16 * i, 16)]))
    copies = [pltpu.make_async_copy(a, b, sem.at[n]) for n, (a, b) in enumerate(pairs)]
    for copy in copies:
        copy.start()
    w1[432:] = jnp.zeros((80, w1.shape[1]), BF16)
    for copy in copies:
        copy.wait()


def in_hbm(*arrays):
    return [pltpu.with_memory_space_constraint(array, pltpu.HBM) for array in arrays]


def fetched_first(k1, b1, g1, b2, g2, b3, latent):
    c1 = k1.shape[4]
    rows = [v.reshape(1, -1) for v in (b1, g1, b2, g2, b3)]
    shapes = [pltpu.VMEM((512, c1), BF16)] + [pltpu.VMEM(v.shape, F32) for v in rows]
    return pl.pallas_call(
        first_weights_kernel,
        out_shape=shapes + [pltpu.VMEM((1,) + latent.shape, BF16)],
        in_specs=[pl.BlockSpec(memory_space=pltpu.HBM)] * 7,
        out_specs=[pl.BlockSpec(memory_space=pltpu.VMEM)] * 7,
        scratch_shapes=[pltpu.SemaphoreType.DMA((33,))],
        compiler_params=pltpu.CompilerParams(vmem_limit_bytes=1024 * 1024),
        cost_estimate=pl.CostEstimate(flops=10000000000, bytes_accessed=40000000, transcendentals=0),
    )(*in_hbm(k1.reshape(3, 9, 16, c1), *rows, latent))


def tap_sums_kernel(i, k2, low, high, full):
    def part(n, _):
        k, at = n // 8, pl.ds(pl.multiple_of(n % 8 * 64, 64), 64)
        a, b, c = [k2[i, j, k, at, :].astype(F32) for j in range(3)]
        ab = a + b
        low[k, at, :] = ab.astype(BF16)
        high[k, at, :] = (b + c).astype(BF16)
        full[k, at, :] = (ab + c).astype(BF16)
        return 0

    lax.fori_loop(0, 24, part, 0)


def tap_sums(k2, i):
    vmem = pl.BlockSpec(memory_space=pltpu.VMEM)
    return pl.pallas_call(
        functools.partial(tap_sums_kernel, i),
        out_shape=[pltpu.VMEM(k2.shape[2:], BF16)] * 3,
        in_specs=[vmem],
        out_specs=[vmem] * 3,
        compiler_params=pltpu.CompilerParams(vmem_limit_bytes=1024 * 1024),
        cost_estimate=pl.CostEstimate(flops=0, bytes_accessed=4_000_000, transcendentals=0),
    )(k2)


def decode_kernel(
    rows_total,
    held,
    received,
    w1,
    b1,
    g1,
    b2,
    g2,
    b3,
    low0,
    high0,
    full0,
    low1,
    high1,
    full1,
    low2,
    high2,
    full2,
    w2,
    w3,
    out_hbm,
    pieces,
    shifted,
    first_act,
    difference,
    upper_sums,
    middle_sums,
    lower_sums,
    second_act,
    outer3,
    middle3,
    line,
    out,
    sem_out,
):
    s = lax.axis_index("seq")
    t = lax.axis_index("tm")
    z, x, y, c = s >> 1, s & 1, t >> 1, t & 1
    n_frames = held.shape[1]
    pieces[:12] = held[...].astype(F32)
    pieces[12:] = received[...].astype(F32)

    def piece_of(row, chunk):
        dz, dx = (row >> 1) - z, (row & 1) ^ x
        dy, dc = (chunk >> 1) ^ y, (chunk & 1) ^ c
        group = jnp.where(dz == 0, 0, jnp.where((dz == 1) == ((z & 1) == 0), 1, 2))
        half = (dx + dy + dc + jnp.where(dz == 0, 0, 1)) & 1
        return half * 12 + group * 4 + 2 * dx + dy

    before = n_frames - 2 - 2 * t
    frame = lax.broadcasted_iota(jnp.int32, (4, n_frames, 128), 1)
    group = lax.broadcasted_iota(jnp.int32, (4, n_frames, 128), 2) // 16
    column32 = lax.broadcasted_iota(jnp.int32, (32, 128), 0)
    for d in range(5):
        row = jnp.clip(s - 2 + d, 0, rows_total - 1)
        block = jnp.stack([pieces[piece_of(row, chunk)] for chunk in range(4)])
        block = jnp.where(frame < before, block[:, :1], pltpu.roll(block, before, 1))
        for bit in (4, 2, 1):
            upper = pltpu.roll(pltpu.roll(block, 8 - bit, 1), 16 * bit, 2)
            lower = upper if bit == 4 else pltpu.roll(pltpu.roll(block, bit, 1), 128 - 16 * bit, 2)
            f, g = (frame & bit) != 0, (group & bit) != 0
            block = jnp.where(f == g, block, jnp.where(f, lower, upper))
        middle = block.reshape(32, 128)
        left = jnp.where(column32 == 0, middle, pltpu.roll(middle, 1, 0))
        right = jnp.where(column32 == 31, middle, pltpu.roll(middle, 31, 0))
        for k, value in enumerate((left, middle, right)):
            for n in range(8):
                turned = pltpu.roll(value, 16 * n, 1) if n else value
                shifted[n, d, k] = turned.astype(BF16)

    lane = lax.broadcasted_iota(jnp.int32, (32, 128), 1)
    near = []
    for r in range(3):
        mine = jnp.clip(s - 1 + r, 0, rows_total - 1)
        near.append([jnp.clip(mine - 1 + j, 0, rows_total - 1) - (s - 2) for j in range(3)])

    def patch(v, r, n):
        value = None
        for tap in range(9):
            if tap * 48 < n * 128 + 128 and tap * 48 + 48 > n * 128:
                part = shifted[(3 * tap - v) % 8, near[r][tap // 3], tap % 3]
                value = part if value is None else jnp.where(lane >= tap * 48 - n * 128, part, value)
        return value

    for v in range(0, 6, 2):
        patches = [
            jnp.concatenate([patch(u, r, n) for n in range(4)], axis=1)
            for u in (v, v + 1)
            for r in range(3)
        ]
        hidden = jnp.dot(
            jnp.concatenate(patches, axis=0), w1[...], preferred_element_type=F32
        )
        act = normed(hidden + b1[...], g1[...]).reshape(2, 3, 32, 512)
        for u in range(2):
            first_act[:, v + u] = act[u]

    v0, v1, v2 = [first_act[r].astype(F32) for r in range(3)]
    difference[0] = (v0 - v1).astype(BF16)
    difference[1] = (v1 - v2).astype(BF16)

    def lhs(ref, r):
        return jnp.concatenate([ref[r, i : i + 4].reshape(128, 512) for i in range(3)], axis=1)

    def side_by_side(taps):
        return jnp.concatenate(
            [jnp.concatenate([tap[k] for tap in of_i for k in range(3)], axis=1) for of_i in taps],
            axis=0,
        )

    middle_sums[...] = jnp.dot(
        lhs(first_act, 1),
        side_by_side([(full,) for full in (full0, full1, full2)]),
        preferred_element_type=F32,
    )
    upper_sums[...] = jnp.dot(
        lhs(difference, 0),
        side_by_side([(low, w2.at[i, 0]) for i, low in enumerate((low0, low1, low2))]),
        preferred_element_type=F32,
    )
    lower_sums[...] = jnp.dot(
        lhs(difference, 1),
        side_by_side([(w2.at[i, 2], high) for i, high in enumerate((high0, high1, high2))]),
        preferred_element_type=F32,
    )

    column = lax.broadcasted_iota(jnp.int32, (4, 32, 256), 1)

    def second_norm(p):
        def sums(k):
            both, own = k * 256, (p % 2 * 3 + k) * 256
            shared = middle_sums[:, both : both + 256]
            if p < 2:
                total = shared + upper_sums[:, own : own + 256]
            else:
                total = shared - lower_sums[:, own : own + 256]
            return total.reshape(4, 32, 256)

        a, b, d = [sums(k) for k in range(3)]
        a_left = jnp.where(column == 0, a, pltpu.roll(a, 1, 1))
        d_right = jnp.where(column == 31, d, pltpu.roll(d, 31, 1))
        second_act[p, 0] = normed(a_left + (b + b2[...]) + d, g2[...])
        second_act[p, 1] = normed(a + (b + b2[...]) + d_right, g2[...])

    for p in range(4):
        second_norm(p)


    def lhs3(rows):
        m = (rows.stop - rows.start) * 128
        return [second_act[rows, :, i : i + 2].reshape(m, 256) for i in range(3)]

    def block3(j, ks):
        return jnp.concatenate(
            [jnp.concatenate([w3[i, j, k] for k in ks], axis=1) for i in range(3)], axis=0
        )

    none = jnp.zeros((768, 128), BF16)
    upper = jnp.concatenate([block3(0, (0, 1, 2)), block3(1, (2,))], axis=1)
    lower = jnp.concatenate([block3(2, (0, 1, 2)), none], axis=1)
    outer3[...] = jnp.dot(
        jnp.concatenate(lhs3(slice(0, 3)) + lhs3(slice(1, 4)), axis=1),
        jnp.concatenate([upper, lower], axis=0),
        preferred_element_type=F32,
    )
    middle3[...] = jnp.dot(
        jnp.concatenate(lhs3(slice(1, 3)), axis=1), block3(1, (0, 1)), preferred_element_type=F32
    )
    narrow = lax.broadcasted_iota(jnp.int32, (32, 128), 0)

    def last(r):
        def part(q, g, k):
            e, m, at = (r + 1) // 2 * 128, r // 2 * 128, (q * 2 + g) * 32
            outer = outer3[e + at : e + at + 32, k * 128 : (k + 1) * 128]
            if k == 2:
                return outer + outer3[m + 128 + at : m + 160 + at, 384:]
            return outer + middle3[m + at : m + at + 32, k * 128 : (k + 1) * 128]

        for g in range(2):
            a0, a1, b0, b1_, d0, d1 = [part(q, g, k) for k in range(3) for q in range(2)]
            a_left = jnp.where(narrow == 0, a0, pltpu.roll(a1, 1, 0))
            d_right = jnp.where(narrow == 31, d1, pltpu.roll(d0, 31, 0))
            columns = (a_left + b0 + d0, a0 + b0 + d1, a0 + b1_ + d1, a1 + b1_ + d_right)
            for u, value in enumerate(columns):
                line[g, pl.ds(u, 32, stride=4), :] = value + b3[...]
            out[g, r] = line[g].astype(BF16)
        pltpu.make_async_copy(out.at[:, r], out_hbm.at[:, r], sem_out.at[r]).start()

    for r in range(4):
        last(r)
    for r in range(4):
        pltpu.make_async_copy(out.at[:, r], out_hbm.at[:, r], sem_out.at[r]).wait()


def per_device(latent, k1, b1, g1, k2, b2, g2, k3, b3):
    frames, lanes = latent.shape
    tm = lax.axis_size("tm")
    rows_total = lax.axis_size("seq")
    c1, c2, c3 = k1.shape[4], k2.shape[4], k3.shape[4]
    held, received, first, sums, k2 = gathered_pieces(
        latent, k1, b1, g1, k2, b2, g2, b3
    )
    vmem = pl.BlockSpec(memory_space=pltpu.VMEM)
    hbm = pl.BlockSpec(memory_space=pltpu.HBM)
    out_frames = frames // tm
    return pl.pallas_call(
        functools.partial(decode_kernel, rows_total),
        out_shape=jax.ShapeDtypeStruct((out_frames, 4, 128, c3), BF16),
        in_specs=[vmem] * 19,
        out_specs=hbm,
        scratch_shapes=[
            pltpu.VMEM((24, frames, 128), F32),
            pltpu.VMEM((8, 5, 3, 32, 128), BF16),
            pltpu.VMEM((3, 6, 32, c1), BF16),
            pltpu.VMEM((2, 6, 32, c1), BF16),
            pltpu.VMEM((128, 6 * c2), F32),
            pltpu.VMEM((128, 3 * c2), F32),
            pltpu.VMEM((128, 6 * c2), F32),
            pltpu.VMEM((4, 2, 4, 32, c2), BF16),
            pltpu.VMEM((384, 4 * c3), F32),
            pltpu.VMEM((256, 2 * c3), F32),
            pltpu.VMEM((2, 128, c3), F32),
            pltpu.VMEM((out_frames, 4, 128, c3), BF16),
            pltpu.SemaphoreType.DMA((4,)),
        ],
        compiler_params=pltpu.CompilerParams(vmem_limit_bytes=12 * 1024 * 1024),
        cost_estimate=pl.CostEstimate(
            flops=4_000_000_000, bytes_accessed=10_000_000, transcendentals=600_000
        ),
    )(held, received, *first, *sums, k2, k3)


def solution(mesh):
    placed = (P(None, AXES), P(), P(), P(), P(), P(), P(), P(), P())
    return jax.shard_map(
        per_device,
        mesh=mesh,
        in_specs=placed,
        out_specs=P("tm", "seq", None, None),
        check_vma=False,
    )
```

```python
import functools

import jax
import jax.numpy as jnp
from jax import lax
from jax.experimental import pallas as pl
from jax.experimental.pallas import tpu as pltpu
from jax.sharding import PartitionSpec as P

F32, BF16 = jnp.float32, jnp.bfloat16
AXES = ("seq", "tm")


def hop(array, partner, seq, tm):
    pairs = []
    for s in range(seq):
        for t in range(tm):
            s2, t2 = partner(s, t)
            pairs.append((s * tm + t, s2 * tm + t2))
    return lax.ppermute(array, AXES, pairs)


def gathered_pieces(latent, k1, b1, g1, k2, b2, g2, b3):
    seq, tm = lax.axis_size("seq"), lax.axis_size("tm")
    assert seq % 2 == 0 and tm == 4

    def z_partner(first):
        def partner(s, t):
            z = s // 2
            other = z + 1 if (z - first) % 2 == 0 else z - 1
            return (s + 2 * (other - z), t ^ 1) if 0 <= other < seq // 2 else (s, t ^ 1)

        return partner

    beside = hop(latent[None], lambda s, t: (s, t ^ 3), seq, tm)
    *first, own = fetched_first(k1, b1, g1, b2, g2, b3, latent)
    beside, own, *first = lax.optimization_barrier((beside, own, *first))
    held = jnp.concatenate([own, beside])
    k2, _ = lax.optimization_barrier((k2, beside))
    across = hop(held, lambda s, t: (s ^ 1, t ^ 1), seq, tm)
    across, *sums0 = lax.optimization_barrier((across, *tap_sums(k2, 0)))
    held = jnp.concatenate([held, across])
    k2, _ = lax.optimization_barrier((k2, across))
    even = hop(held, z_partner(0), seq, tm)
    odd = hop(held, z_partner(1), seq, tm)
    odd, even, *sums1 = lax.optimization_barrier((odd, even, *tap_sums(k2, 1)))
    held = jnp.concatenate([held, even, odd])
    k2, _ = lax.optimization_barrier((k2, even))
    received = hop(held, lambda s, t: (s, t ^ 1), seq, tm)
    sums2 = tap_sums(k2, 2)
    return held, received, first, [*sums0, *sums1, *sums2], k2


def normed(hidden, gain):
    factor = lax.rsqrt(jnp.mean(hidden * hidden, axis=-1, keepdims=True) + 1e-06)
    half = hidden * (0.5 * factor) * gain
    return (half + half * jnp.tanh(half)).astype(BF16)


def first_weights_kernel(
    k1, b1_in, g1_in, b2_in, g2_in, b3_in, latent, w1, b1, g1, b2, g2, b3, own, sem
):
    pairs = [(b1_in, b1), (g1_in, g1), (b2_in, b2), (g2_in, g2), (b3_in, b3)]
    pairs.append((latent, own.at[0]))
    for i in range(3):
        pairs.append((k1.at[i], w1.at[pl.ds(0, 9), pl.ds(16 * (1 + i), 16)]))
    copies = [pltpu.make_async_copy(a, b, sem.at[n]) for n, (a, b) in enumerate(pairs)]
    for copy in copies:
        copy.start()
    zeros = jnp.zeros((9, 16, w1.shape[2]), BF16)
    w1[:9, :16] = zeros
    w1[:9, 64:] = zeros
    w1[9] = jnp.zeros(w1.shape[1:], BF16)
    for copy in copies:
        copy.wait()


def in_hbm(*arrays):
    return [pltpu.with_memory_space_constraint(array, pltpu.HBM) for array in arrays]


def fetched_first(k1, b1, g1, b2, g2, b3, latent):
    c1 = k1.shape[4]
    rows = [v.reshape(1, -1) for v in (b1, g1, b2, g2, b3)]
    shapes = [pltpu.VMEM((10, 80, c1), BF16)] + [pltpu.VMEM(v.shape, F32) for v in rows]
    return pl.pallas_call(
        first_weights_kernel,
        out_shape=shapes + [pltpu.VMEM((1,) + latent.shape, BF16)],
        in_specs=[pl.BlockSpec(memory_space=pltpu.HBM)] * 7,
        out_specs=[pl.BlockSpec(memory_space=pltpu.VMEM)] * 7,
        scratch_shapes=[pltpu.SemaphoreType.DMA((9,))],
        compiler_params=pltpu.CompilerParams(vmem_limit_bytes=1024 * 1024),
        cost_estimate=pl.CostEstimate(flops=10000000000, bytes_accessed=40000000, transcendentals=0),
    )(*in_hbm(k1.reshape(3, 9, 16, c1), *rows, latent))


def tap_sums_kernel(i, k2, low, high, full):
    def part(n, _):
        k, at = n // 8, pl.ds(pl.multiple_of(n % 8 * 64, 64), 64)
        a, b, c = [k2[i, j, k, at, :].astype(F32) for j in range(3)]
        ab = a + b
        low[k, at, :] = ab.astype(BF16)
        high[k, at, :] = (b + c).astype(BF16)
        full[k, at, :] = (ab + c).astype(BF16)
        return 0

    lax.fori_loop(0, 24, part, 0)


def tap_sums(k2, i):
    vmem = pl.BlockSpec(memory_space=pltpu.VMEM)
    return pl.pallas_call(
        functools.partial(tap_sums_kernel, i),
        out_shape=[pltpu.VMEM(k2.shape[2:], BF16)] * 3,
        in_specs=[vmem],
        out_specs=[vmem] * 3,
        compiler_params=pltpu.CompilerParams(vmem_limit_bytes=1024 * 1024),
        cost_estimate=pl.CostEstimate(flops=0, bytes_accessed=4_000_000, transcendentals=0),
    )(k2)


def decode_kernel(
    rows_total,
    held,
    received,
    w1,
    b1,
    g1,
    b2,
    g2,
    b3,
    low0,
    high0,
    full0,
    low1,
    high1,
    full1,
    low2,
    high2,
    full2,
    w2,
    w3,
    out_hbm,
    pieces,
    shifted,
    patches,
    first_act,
    difference,
    upper_sums,
    middle_sums,
    lower_sums,
    second_act,
    outer3,
    middle3,
    line,
    out,
    sem_out,
):
    s = lax.axis_index("seq")
    t = lax.axis_index("tm")
    z, x, y, c = s >> 1, s & 1, t >> 1, t & 1
    n_frames = held.shape[1]
    pieces[:12] = held[...].astype(F32)
    pieces[12:] = received[...].astype(F32)

    def piece_of(row, chunk):
        dz, dx = (row >> 1) - z, (row & 1) ^ x
        dy, dc = (chunk >> 1) ^ y, (chunk & 1) ^ c
        group = jnp.where(dz == 0, 0, jnp.where((dz == 1) == ((z & 1) == 0), 1, 2))
        half = (dx + dy + dc + jnp.where(dz == 0, 0, 1)) & 1
        return half * 12 + group * 4 + 2 * dx + dy

    before = n_frames - 2 - 2 * t
    frame = lax.broadcasted_iota(jnp.int32, (4, n_frames, 128), 1)
    group = lax.broadcasted_iota(jnp.int32, (4, n_frames, 128), 2) // 16
    column32 = lax.broadcasted_iota(jnp.int32, (32, 128), 0)
    for d in range(5):
        row = jnp.clip(s - 2 + d, 0, rows_total - 1)
        block = jnp.stack([pieces[piece_of(row, chunk)] for chunk in range(4)])
        block = jnp.where(frame < before, block[:, :1], pltpu.roll(block, before, 1))
        for bit in (4, 2, 1):
            upper = pltpu.roll(pltpu.roll(block, 8 - bit, 1), 16 * bit, 2)
            lower = upper if bit == 4 else pltpu.roll(pltpu.roll(block, bit, 1), 128 - 16 * bit, 2)
            f, g = (frame & bit) != 0, (group & bit) != 0
            block = jnp.where(f == g, block, jnp.where(f, lower, upper))
        middle = block.reshape(32, 128)
        left = jnp.where(column32 == 0, middle, pltpu.roll(middle, 1, 0))
        right = jnp.where(column32 == 31, middle, pltpu.roll(middle, 31, 0))
        for k, value in enumerate((left, middle, right)):
            for n, turn in enumerate((0, 96, 64, 32)):
                turned = pltpu.roll(value, turn, 1) if turn else value
                shifted[n, d, k] = turned.astype(BF16)

    low = lax.broadcasted_iota(jnp.int32, (32, 128), 1) < 64
    for r in range(3):
        mine = jnp.clip(s - 1 + r, 0, rows_total - 1)
        d = [jnp.clip(mine - 1 + j, 0, rows_total - 1) - (s - 2) for j in range(3)]
        for n in range(5):
            first, second = 2 * n, min(2 * n + 1, 8)
            for v in range(3):
                one = shifted[v, d[first // 3], first % 3]
                two = shifted[(v + 2) % 4, d[second // 3], second % 3]
                patches[v, r, :, n * 128 : (n + 1) * 128] = jnp.where(low, one, two)

    for b in range(2):
        window = slice(16 - 16 * b, 80 - 16 * b)
        hidden = jnp.dot(
            patches[...].reshape(288, 640),
            jnp.concatenate([w1[n, window] for n in range(10)], axis=0),
            preferred_element_type=F32,
        )
        act = normed(hidden + b1[...], g1[...]).reshape(3, 3, 32, 512)
        for v in range(3):
            first_act[:, 2 * v + b] = act[v]

    v0, v1, v2 = [first_act[r].astype(F32) for r in range(3)]
    difference[0] = (v0 - v1).astype(BF16)
    difference[1] = (v1 - v2).astype(BF16)

    def lhs(ref, r):
        return jnp.concatenate([ref[r, i : i + 4].reshape(128, 512) for i in range(3)], axis=1)

    def side_by_side(taps):
        return jnp.concatenate(
            [jnp.concatenate([tap[k] for tap in of_i for k in range(3)], axis=1) for of_i in taps],
            axis=0,
        )

    middle_sums[...] = jnp.dot(
        lhs(first_act, 1),
        side_by_side([(full,) for full in (full0, full1, full2)]),
        preferred_element_type=F32,
    )
    upper_sums[...] = jnp.dot(
        lhs(difference, 0),
        side_by_side([(low, w2.at[i, 0]) for i, low in enumerate((low0, low1, low2))]),
        preferred_element_type=F32,
    )
    lower_sums[...] = jnp.dot(
        lhs(difference, 1),
        side_by_side([(w2.at[i, 2], high) for i, high in enumerate((high0, high1, high2))]),
        preferred_element_type=F32,
    )

    column = lax.broadcasted_iota(jnp.int32, (4, 32, 256), 1)

    def second_norm(p):
        def sums(k):
            both, own = k * 256, (p % 2 * 3 + k) * 256
            shared = middle_sums[:, both : both + 256]
            if p < 2:
                total = shared + upper_sums[:, own : own + 256]
            else:
                total = shared - lower_sums[:, own : own + 256]
            return total.reshape(4, 32, 256)

        a, b, d = [sums(k) for k in range(3)]
        a_left = jnp.where(column == 0, a, pltpu.roll(a, 1, 1))
        d_right = jnp.where(column == 31, d, pltpu.roll(d, 31, 1))
        second_act[p, 0] = normed(a_left + (b + b2[...]) + d, g2[...])
        second_act[p, 1] = normed(a + (b + b2[...]) + d_right, g2[...])

    for p in range(4):
        second_norm(p)


    def lhs3(rows):
        m = (rows.stop - rows.start) * 128
        return [second_act[rows, :, i : i + 2].reshape(m, 256) for i in range(3)]

    def block3(j, ks):
        return jnp.concatenate(
            [jnp.concatenate([w3[i, j, k] for k in ks], axis=1) for i in range(3)], axis=0
        )

    none = jnp.zeros((768, 128), BF16)
    upper = jnp.concatenate([block3(0, (0, 1, 2)), block3(1, (2,))], axis=1)
    lower = jnp.concatenate([block3(2, (0, 1, 2)), none], axis=1)
    outer3[...] = jnp.dot(
        jnp.concatenate(lhs3(slice(0, 3)) + lhs3(slice(1, 4)), axis=1),
        jnp.concatenate([upper, lower], axis=0),
        preferred_element_type=F32,
    )
    middle3[...] = jnp.dot(
        jnp.concatenate(lhs3(slice(1, 3)), axis=1), block3(1, (0, 1)), preferred_element_type=F32
    )
    narrow = lax.broadcasted_iota(jnp.int32, (32, 128), 0)

    def last(r):
        def part(q, g, k):
            e, m, at = (r + 1) // 2 * 128, r // 2 * 128, (q * 2 + g) * 32
            outer = outer3[e + at : e + at + 32, k * 128 : (k + 1) * 128]
            if k == 2:
                return outer + outer3[m + 128 + at : m + 160 + at, 384:]
            return outer + middle3[m + at : m + at + 32, k * 128 : (k + 1) * 128]

        for g in range(2):
            a0, a1, b0, b1_, d0, d1 = [part(q, g, k) for k in range(3) for q in range(2)]
            a_left = jnp.where(narrow == 0, a0, pltpu.roll(a1, 1, 0))
            d_right = jnp.where(narrow == 31, d1, pltpu.roll(d0, 31, 0))
            columns = (a_left + b0 + d0, a0 + b0 + d1, a0 + b1_ + d1, a1 + b1_ + d_right)
            for u, value in enumerate(columns):
                line[g, pl.ds(u, 32, stride=4), :] = value + b3[...]
            out[g, r] = line[g].astype(BF16)
        pltpu.make_async_copy(out.at[:, r], out_hbm.at[:, r], sem_out.at[r]).start()

    for r in range(4):
        last(r)
    for r in range(4):
        pltpu.make_async_copy(out.at[:, r], out_hbm.at[:, r], sem_out.at[r]).wait()


def per_device(latent, k1, b1, g1, k2, b2, g2, k3, b3):
    frames, lanes = latent.shape
    tm = lax.axis_size("tm")
    rows_total = lax.axis_size("seq")
    c1, c2, c3 = k1.shape[4], k2.shape[4], k3.shape[4]
    held, received, first, sums, k2 = gathered_pieces(
        latent, k1, b1, g1, k2, b2, g2, b3
    )
    vmem = pl.BlockSpec(memory_space=pltpu.VMEM)
    hbm = pl.BlockSpec(memory_space=pltpu.HBM)
    out_frames = frames // tm
    return pl.pallas_call(
        functools.partial(decode_kernel, rows_total),
        out_shape=jax.ShapeDtypeStruct((out_frames, 4, 128, c3), BF16),
        in_specs=[vmem] * 19,
        out_specs=hbm,
        scratch_shapes=[
            pltpu.VMEM((24, frames, 128), F32),
            pltpu.VMEM((4, 5, 3, 32, 128), BF16),
            pltpu.VMEM((3, 3, 32, 640), BF16),
            pltpu.VMEM((3, 6, 32, c1), BF16),
            pltpu.VMEM((2, 6, 32, c1), BF16),
            pltpu.VMEM((128, 6 * c2), F32),
            pltpu.VMEM((128, 3 * c2), F32),
            pltpu.VMEM((128, 6 * c2), F32),
            pltpu.VMEM((4, 2, 4, 32, c2), BF16),
            pltpu.VMEM((384, 4 * c3), F32),
            pltpu.VMEM((256, 2 * c3), F32),
            pltpu.VMEM((2, 128, c3), F32),
            pltpu.VMEM((out_frames, 4, 128, c3), BF16),
            pltpu.SemaphoreType.DMA((4,)),
        ],
        compiler_params=pltpu.CompilerParams(vmem_limit_bytes=12 * 1024 * 1024),
        cost_estimate=pl.CostEstimate(
            flops=4_000_000_000, bytes_accessed=10_000_000, transcendentals=600_000
        ),
    )(held, received, *first, *sums, k2, k3)


def solution(mesh):
    placed = (P(None, AXES), P(), P(), P(), P(), P(), P(), P(), P())
    return jax.shard_map(
        per_device,
        mesh=mesh,
        in_specs=placed,
        out_specs=P("tm", "seq", None, None),
        check_vma=False,
    )
```
